32 devices in a mesh: wide: 16 (over z, x, core), dp: 2 (over y).
Axes of the slice: x: 2, y: 2, z: 4, core: 2. Of those that a mesh axis runs over, the one named last changes fastest.
Arguments:
- queries: bfloat16 [16384, 4096], P(('wide', 'dp')), may hold values from -20 to 20
- teacher_queries: bfloat16 [16384, 4096], P(('wide', 'dp')), may hold values from -6 to 6
- passages: bfloat16 [256, 4096], P('wide'), may hold values from -6 to 6
- bank_student: bfloat16 [4096, 4096], P('wide'), may hold values from -6 to 6
- bank_teacher: bfloat16 [4096, 4096], P('wide'), may hold values from -6 to 6
- owner: int32 [2], P('dp'), may hold values from 0 to 15
- positives: int32 [16384], P(('wide', 'dp')), may hold values from 0 to 255
- keep_mask: int32 [16384, 256], P(('wide', 'dp')), may hold values 0 or 1
Outputs:
- row_loss: float32 [16384], P(('wide', 'dp'))
- query_grad: bfloat16 [16384, 4096], P(('wide', 'dp'))
- passage_grad: float32 [256, 4096], P('wide')
The draws below stay inside these ranges and needn't reach their ends.
All inputs are finite; a program needn't handle non-finite values. No bound on the sum of `keep_mask` on one device may be relied on, other than what follows from the above.
Results may differ from the reference program's by a relative error of at most 0.0033.
Values may be sent and summed in bfloat16 or wider, within the bound.
No kernel may reach another device: no remote copies, remote signals or barrier semaphores. Data moves between devices by JAX's collectives and lax.ppermute only.
A program may use at most 128 MiB of HBM per device.

```python
import math
import jax
import jax.numpy as jnp
from jax import lax

E = 4096
QDEV = 512
POOL = 256
NP = 256
QN = 16384
BANK = 4096
N_WIDE = 16
N_DP = 2


def draw_pair(key):
    base = jax.random.fold_in(key, 11)
    key_a, key_b = jax.random.split(base, 2)
    passages = jnp.clip(jax.random.normal(key_a, (NP, E), jnp.float32), -4.0, 4.0)
    queries = jnp.clip(jax.random.normal(key_b, (QN, E), jnp.float32), -4.0, 4.0)
    return (queries, passages)


def draw_queries(key, part):
    return draw_pair(key)[0].astype(jnp.bfloat16)


def draw_passages(key, part):
    return draw_pair(key)[1].astype(jnp.bfloat16)


def place_ends(drawn, stream_key, smallest, high):
    longest = drawn.shape.index(max(drawn.shape))
    spots = []
    for shift in (0, 1):
        where = [jax.random.randint(jax.random.fold_in(stream_key, axis), (), 0, length) for axis, length in enumerate(drawn.shape)]
        where[longest] = (where[longest] + shift) % drawn.shape[longest]
        spots.append(tuple(where))
    return drawn.at[spots[0]].set(smallest).at[spots[1]].set(high)


def block_levels(rng, extent, shards, least, top_value):
    factor_of, own = 1.0, jax.random.fold_in(rng, 6)
    for dim, parts in shards:
        steps = jnp.exp(jax.random.uniform(jax.random.fold_in(own, dim), (parts,), jnp.float32, least / len(shards), top_value / len(shards)))
        factor_of = factor_of * jnp.repeat(steps, extent[dim] // parts).reshape([-1 if axis == dim else 1 for axis in range(len(extent))])
    return factor_of


def gaussian(own_key, extent, scale, reach, cuts=(), held_as=jnp.bfloat16):
    entries = scale * jax.random.normal(own_key, extent, jnp.float32)
    if cuts:
        entries = entries * block_levels(own_key, extent, cuts, -0.22, 0.18)
    return jnp.clip(entries, -reach, reach).astype(held_as)


def setup_inputs(seed: int = 0) -> dict:
    key_list = jax.random.split(jax.random.key(seed), 9)
    queries = draw_queries(jax.random.fold_in(key_list[8], 71), 0)
    teacher_queries = gaussian(key_list[1], (QN, E), 1.0, 6.0, ((0, 32),))
    passages = draw_passages(jax.random.fold_in(key_list[8], 71), 0)
    bank_student = gaussian(key_list[3], (BANK, E), 1.0, 6.0, ((0, 16),))
    bank_teacher = gaussian(key_list[4], (BANK, E), 1.0, 6.0, ((0, 16),))
    owner = jax.random.randint(key_list[5], (N_DP,), 0, N_WIDE).astype(jnp.int32)
    positives = place_ends(jax.random.randint(key_list[6], (QN,), 0, NP), jax.random.fold_in(key_list[6], 1), 0, NP - 1).astype(jnp.int32)
    keep_mask = place_ends((jax.random.randint(key_list[7], (QN, POOL), 0, 2) < 1).astype(jnp.int32), jax.random.fold_in(key_list[7], 1), 0, 1)
    return {"queries": queries, "teacher_queries": teacher_queries, "passages": passages, "bank_student": bank_student, "bank_teacher": bank_teacher, "owner": owner, "positives": positives, "keep_mask": keep_mask}


def reference(queries, teacher_queries, passages, bank_student, bank_teacher, owner, positives, keep_mask):
    scale = 2.0 / math.sqrt(E)
    count = QN // QDEV
    query_blocks = queries.reshape(count, QDEV, E)
    teacher_blocks = teacher_queries.reshape(count, QDEV, E)
    pos_blocks = positives.reshape(count, QDEV)
    mask_blocks = keep_mask.reshape(count, QDEV, POOL)
    block_ids = jnp.arange(count, dtype=jnp.int32)
    columns = jnp.arange(NP, dtype=jnp.int32)

    def one_block(carry, items):
        query, teacher, pos, keep, block_id = items
        replica = (block_id % N_DP).astype(jnp.int32)
        first = (owner[replica].astype(jnp.int32) * POOL).astype(jnp.int32)
        pool_s = lax.dynamic_slice_in_dim(bank_student, first, POOL, 0)
        pool_t = lax.dynamic_slice_in_dim(bank_teacher, first, POOL, 0)
        zp = jnp.dot(query, passages.T, preferred_element_type=jnp.float32) * scale
        zq = jnp.dot(query, pool_s.T, preferred_element_type=jnp.float32) * scale
        tt = jnp.dot(teacher, pool_t.T, preferred_element_type=jnp.float32) * scale
        weight = keep.astype(jnp.float32) * jax.nn.sigmoid(-tt)
        top = jnp.maximum(lax.optimization_barrier(jnp.max(zp, axis=1)), lax.optimization_barrier(jnp.max(zq, axis=1)))
        total = lax.optimization_barrier(jnp.sum(jnp.exp(zp - top[:, None]), axis=1)) + lax.optimization_barrier(jnp.sum(weight * jnp.exp(zq - top[:, None]), axis=1))
        lse = top + jnp.log(total)
        hit = (columns[None, :] == pos[:, None]).astype(jnp.float32)
        loss = lse - lax.optimization_barrier(jnp.sum(zp * hit, axis=1))
        grad_p = (jnp.exp(zp - lse[:, None]) - hit).astype(jnp.bfloat16)
        grad_q = (weight * jnp.exp(zq - lse[:, None])).astype(jnp.bfloat16)
        qgrad = (jnp.dot(grad_p, passages, preferred_element_type=jnp.float32) + jnp.dot(grad_q, pool_s, preferred_element_type=jnp.float32)) * scale
        carry = carry + lax.dot_general(grad_p, query, (((0,), (0,)), ((), ())), preferred_element_type=jnp.float32)
        return (carry, (loss, qgrad.astype(jnp.bfloat16)))
    start = jnp.zeros((NP, E), jnp.float32)
    summed, (losses, qgrads) = lax.scan(one_block, start, (query_blocks, teacher_blocks, pos_blocks, mask_blocks, block_ids))
    return (losses.reshape(QN), qgrads.reshape(QN, E), summed * scale)
```

```python
import math

import jax
import jax.numpy as jnp
from jax import lax
from jax.sharding import PartitionSpec as P

E = 4096
CHUNKS = 4


def ring_order(n_chip):
    nz = n_chip // 2
    return [2 * z for z in range(nz)] + [2 * z + 1 for z in reversed(range(nz))]


def ring_pairs(n_chip):
    order = ring_order(n_chip)
    pairs = []
    for i, chip in enumerate(order):
        pairs.append((2 * chip, 2 * order[(i + 1) % n_chip]))
        pairs.append((2 * chip + 1, 2 * order[(i - 1) % n_chip] + 1))
    return pairs


def pool_halves(bank_s, bank_t, owner, index, core):
    n_dev = lax.axis_size("wide")
    n_chip = n_dev // 2
    half = bank_s.shape[0] // 2
    step_rows = half // CHUNKS
    order = ring_order(n_chip)
    place = jnp.array([order.index(c) for c in range(n_chip)], jnp.int32)
    away = place[index // 2] - place[owner // 2]
    distance = jnp.where(core == 0, away, -away) % n_chip
    own_chip = owner // 2 == index // 2
    own_core = owner == index
    swap = [(i, i ^ 1) for i in range(n_dev)]
    pairs = ring_pairs(n_chip)
    mine = []
    for bank in (bank_s, bank_t):
        got = lax.ppermute(
            lax.dynamic_slice_in_dim(bank, (1 - core) * half, half, 0), "wide", swap
        )
        mine.append(
            jnp.where(own_core, lax.dynamic_slice_in_dim(bank, core * half, half, 0), got)
        )
    spare = jnp.zeros((step_rows, bank_s.shape[1]), bank_s.dtype)
    pools = [jnp.concatenate([m, spare], 0) for m in mine]
    moving = [m[:step_rows] for m in mine]
    for t in range(CHUNKS + n_chip - 2):
        slot = t - (distance - 1)
        slot = jnp.where(own_chip | (slot > CHUNKS), CHUNKS, jnp.maximum(slot, 0))
        for i in range(2):
            got = lax.ppermute(moving[i], "wide", pairs)
            pools[i] = lax.dynamic_update_slice_in_dim(pools[i], got, slot * step_rows, 0)
            if t + 1 < CHUNKS:
                got = jnp.where(own_chip, mine[i][(t + 1) * step_rows : (t + 2) * step_rows], got)
            moving[i] = got
    return [p[:half] for p in pools]


def dot_t(a, b):
    return lax.dot_general(a, b, (((1,), (1,)), ((), ())), preferred_element_type=jnp.float32)


def body(
    queries, teacher_queries, passages, bank_student, bank_teacher, owner, positives, keep_mask
):
    scale = 2.0 / math.sqrt(E)
    n_dev = lax.axis_size("wide")
    n_chip = n_dev // 2
    n_dp = lax.axis_size("dp")
    index = lax.axis_index("wide")
    replica = lax.axis_index("dp")
    core = index % 2
    block = passages.shape[0]
    n_pass = block * n_dev
    parts = 2 if n_dp == 2 else 1
    sub = block // parts
    swap = [(i, i ^ 1) for i in range(n_dev)]
    across = [(0, 1), (1, 0)]

    gathered = lax.all_gather(passages, "wide", axis=0, tiled=True)
    split = gathered.reshape(n_chip, 2, parts, sub, E)
    split = jnp.where(core == 0, split[:, ::-1], split)
    if parts == 2:
        split = jnp.where(replica == 0, split[:, :, ::-1], split)
    pieces = split.transpose(1, 2, 0, 3, 4).reshape(n_pass, E)
    chip_of = positives // (2 * block)
    core_of = (positives // block) % 2
    half_of = (positives // sub) % parts
    core_of = jnp.where(core == 0, 1 - core_of, core_of)
    if parts == 2:
        half_of = jnp.where(replica == 0, 1 - half_of, half_of)
    column = ((core_of * parts + half_of) * n_chip + chip_of) * sub + positives % sub

    zp = dot_t(queries, pieces) * scale
    top_p = jnp.max(zp, axis=1)

    pool_s, pool_t = pool_halves(bank_student, bank_teacher, owner[0], index, core)
    other_s = lax.ppermute(pool_s, "wide", swap)
    other_t = lax.ppermute(pool_t, "wide", swap)
    half = pool_s.shape[0]
    keep = jnp.where(core == 0, keep_mask, jnp.roll(keep_mask, half, 1)).astype(jnp.float32)
    zq = jnp.concatenate([dot_t(queries, pool_s), dot_t(queries, other_s)], 1) * scale
    tt = jnp.concatenate([dot_t(teacher_queries, pool_t), dot_t(teacher_queries, other_t)], 1) * scale
    weight = keep * jax.nn.sigmoid(-tt)
    top = jnp.maximum(top_p, jnp.max(zq, axis=1))
    total = jnp.sum(jnp.exp(zp - top[:, None]), axis=1) + jnp.sum(
        weight * jnp.exp(zq - top[:, None]), axis=1
    )
    lse = top + jnp.log(total)
    hit = (jnp.arange(n_pass, dtype=jnp.int32)[None, :] == column[:, None]).astype(jnp.float32)
    row_loss = lse - jnp.sum(zp * hit, axis=1)
    grad_p = (jnp.exp(zp - lse[:, None]) - hit).astype(jnp.bfloat16)
    grad_q = (weight * jnp.exp(zq - lse[:, None])).astype(jnp.bfloat16)

    def terms(columns):
        return lax.dot_general(
            columns, queries, (((0,), (0,)), ((), ())), preferred_element_type=jnp.float32
        )

    mid = n_pass // 2
    sent = lax.ppermute(terms(grad_p[:, :mid]).astype(jnp.bfloat16), "wide", swap)
    sums = terms(grad_p[:, mid:]) + sent.astype(jnp.float32)
    if parts == 2:
        sent = lax.ppermute(sums[: mid // 2].astype(jnp.bfloat16), "dp", across)
        sums = sums[mid // 2 :] + sent.astype(jnp.float32)
    sums = sums.reshape(n_chip, sub, E)
    chip = index // 2
    own = lax.dynamic_slice_in_dim(sums, chip, 1, 0)[0]
    packed = sums.astype(jnp.bfloat16)
    for j in range(1, n_chip):
        part = lax.dynamic_slice_in_dim(packed, chip ^ j, 1, 0)[0]
        got = lax.ppermute(part, "wide", [(i, i ^ (2 * j)) for i in range(n_dev)])
        own = own + got.astype(jnp.float32)
    if parts == 2:
        own = own * scale
        got = lax.ppermute(own, "dp", across)
        passage_grad = jnp.where(
            replica == 0, jnp.concatenate([own, got], 0), jnp.concatenate([got, own], 0)
        )
    else:
        passage_grad = lax.psum(own, "dp") * scale

    qgrad = (
        jnp.dot(grad_p, pieces, preferred_element_type=jnp.float32)
        + jnp.dot(grad_q[:, :half], pool_s, preferred_element_type=jnp.float32)
        + jnp.dot(grad_q[:, half:], other_s, preferred_element_type=jnp.float32)
    )
    query_grad = (qgrad * scale).astype(jnp.bfloat16)
    return (row_loss, query_grad, passage_grad)


def solution(mesh):
    placed = (
        P(("wide", "dp"), None),
        P(("wide", "dp"), None),
        P("wide", None),
        P("wide", None),
        P("wide", None),
        P("dp"),
        P(("wide", "dp")),
        P(("wide", "dp"), None),
    )
    return jax.shard_map(
        body,
        mesh=mesh,
        in_specs=placed,
        out_specs=(P(("wide", "dp")), P(("wide", "dp"), None), P("wide", None)),
        check_vma=False,
    )
```

```python
import math

import jax
import jax.numpy as jnp
from jax import lax
from jax.sharding import PartitionSpec as P

STEP = 24


def ring_order(n_chip):
    nz = n_chip // 2
    return [2 * z for z in range(nz)] + [2 * z + 1 for z in reversed(range(nz))]


def ring_pairs(n_chip):
    order = ring_order(n_chip)
    pairs = []
    for i, chip in enumerate(order):
        pairs.append((2 * chip, 2 * order[(i + 1) % n_chip]))
        pairs.append((2 * chip + 1, 2 * order[(i - 1) % n_chip] + 1))
    return pairs


def swap_pairs(n, bit):
    return [(i, i ^ bit) for i in range(n)]


def rows_at(x, tile, count):
    return lax.dynamic_slice_in_dim(x, tile * 8, count, 0)


def put_rows(x, rows, tile):
    return lax.dynamic_update_slice_in_dim(x, rows, tile * 8, 0)


def gather_rows(bank_s, bank_t, passages, owner, index, core):
    n_dev = lax.axis_size("wide")
    n_chip = n_dev // 2
    pool, width = bank_s.shape
    sub = passages.shape[0]
    far = n_chip // 2
    cut = 4 * STEP if pool >= 8 * STEP else pool // 2
    n_cut = cut // STEP
    n_shared = -(-(pool - 2 * cut) // STEP)
    chunks = n_cut + n_shared
    rounds = max(n_cut + n_chip - 2, chunks + far - 1)
    chip = index // 2

    def place(c):
        return jnp.where(c % 2 == 0, c // 2, n_chip - 1 - c // 2)

    def chip_at(p):
        return jnp.where(p < n_chip // 2, 2 * p, 2 * (n_chip - 1 - p) + 1)

    here = place(chip)
    turn = 1 - 2 * core
    distance = (turn * (here - place(owner // 2)) + n_chip) % n_chip
    own_chip = owner // 2 == chip
    own_core = owner == index
    near = distance <= far
    swap = swap_pairs(n_dev, 1)
    pairs = ring_pairs(n_chip)
    banks = (bank_s, bank_t)

    def start_of(j, side):
        shared = jnp.minimum((2 * cut + (j - n_cut) * STEP) // 8, (pool - STEP) // 8)
        return jnp.where(j < n_cut, side * (cut // 8) + j * (STEP // 8), shared)

    def handed(held, start, count):
        return [lax.ppermute(rows_at(b, start, count), "wide", swap) for b in held]

    early = 2 * STEP
    first = handed(banks, (1 - core) * (cut // 8), early)
    mine = [
        jnp.where(own_core, rows_at(b, core * (cut // 8), early), g) for b, g in zip(banks, first)
    ]

    def own_rows(i, j):
        if j < 2:
            return mine[i][j * STEP : (j + 1) * STEP]
        if j < n_cut:
            return later[i][(j - 2) * STEP : (j - 1) * STEP]
        at = min((j - n_cut) * STEP, pool - 2 * cut - STEP) + cut - early
        return later[i][at : at + STEP]

    pools = [jnp.zeros_like(bank_s), jnp.zeros_like(bank_t)]
    moving = [own_rows(i, 0) for i in range(2)]
    rows = put_rows(jnp.zeros((n_chip * sub, width), passages.dtype), passages, 0)
    riding = passages
    arrived = [[], []]
    for t in range(rounds):
        slot = jnp.where(own_chip, t, t - (distance - 1))
        take = (slot >= 0) & (slot < chunks)
        where_to = start_of(jnp.clip(slot, 0, chunks - 1), core)
        for i in range(2):
            ride = i == 0 and t < n_chip - 1
            sent = jnp.concatenate([moving[i], riding], 0) if ride else moving[i]
            if t >= 2:
                sent, arrived[1 - i][t - 2] = lax.optimization_barrier((sent, arrived[1 - i][t - 2]))
            got = lax.ppermute(sent, "wide", pairs)
            arrived[i].append(got)
            if ride:
                riding = got[STEP:]
                got = got[:STEP]
                origin = chip_at((here - turn * (t + 1) + n_chip) % n_chip)
                rows = put_rows(rows, riding, (origin ^ chip) * (sub // 8))
            kept = jnp.where(own_chip, own_rows(i, t), got) if t < chunks else got
            pools[i] = put_rows(
                pools[i], jnp.where(take, kept, rows_at(pools[i], where_to, STEP)), where_to
            )
            moving[i] = got
            if t + 1 < chunks:
                moving[i] = jnp.where(own_chip, own_rows(i, t + 1), got)
        if t == 0:
            held, arrived[0][0] = lax.optimization_barrier((banks, arrived[0][0]))
            second = handed(held, (1 - core) * (cut // 8) + early // 8, cut - early)
            third = handed(held, 2 * cut // 8, pool - 2 * cut)
            later = [
                jnp.concatenate(
                    [
                        jnp.where(own_core, rows_at(b, core * (cut // 8) + early // 8, cut - early), g),
                        jnp.where(own_core, b[2 * cut :], h),
                    ],
                    0,
                )
                for b, g, h in zip(held, second, third)
            ]
    full = []
    for p in pools:
        ring = rows_at(p, core * (cut // 8), cut)
        tail = p[2 * cut :]
        ring_other = lax.ppermute(ring, "wide", swap)
        tail_other = lax.ppermute(tail, "wide", swap)
        low = jnp.where(core == 0, ring, ring_other)
        high = jnp.where(core == 0, ring_other, ring)
        full.append(jnp.concatenate([low, high, jnp.where(near, tail, tail_other)], 0))
    return full[0], full[1], rows


def dot_t(a, b):
    return lax.dot_general(a, b, (((1,), (1,)), ((), ())), preferred_element_type=jnp.float32)


def body(
    queries, teacher_queries, passages, bank_student, bank_teacher, owner, positives, keep_mask
):
    n_dev = lax.axis_size("wide")
    n_chip = n_dev // 2
    n_dp = lax.axis_size("dp")
    index = lax.axis_index("wide")
    replica = lax.axis_index("dp")
    core = index % 2
    chip = index // 2
    block, width = passages.shape
    scale = 2.0 / math.sqrt(width)
    n_pass = block * n_dev
    parts = 2 if n_dp == 2 else 1
    sub = block // parts
    swap = swap_pairs(n_dev, 1)
    across = [(0, 1), (1, 0)]

    part = rows_at(passages, replica * (sub // 8), sub) if parts == 2 else passages
    pool_s, pool_t, rows = gather_rows(bank_student, bank_teacher, part, owner[0], index, core)
    if parts == 2:
        rows = jnp.concatenate([rows, lax.ppermute(rows, "dp", across)], 0)
    pieces = jnp.concatenate([rows, lax.ppermute(rows, "wide", swap)], 0)
    chip_of = (positives // (2 * block)) ^ chip
    core_of = ((positives // block) % 2) ^ core
    half_of = (positives // sub) % parts
    if parts == 2:
        half_of = half_of ^ replica
    column = ((core_of * parts + half_of) * n_chip + chip_of) * sub + positives % sub

    zp = dot_t(queries, pieces) * scale

    keep = keep_mask.astype(jnp.float32)
    zq = dot_t(queries, pool_s) * scale
    tt = dot_t(teacher_queries, pool_t) * scale
    weight = keep * jax.nn.sigmoid(-tt)
    top = jnp.maximum(jnp.max(zp, axis=1), jnp.max(zq, axis=1))
    total = jnp.sum(jnp.exp(zp - top[:, None]), axis=1) + jnp.sum(
        weight * jnp.exp(zq - top[:, None]), axis=1
    )
    lse = top + jnp.log(total)
    hit = (jnp.arange(n_pass, dtype=jnp.int32)[None, :] == column[:, None]).astype(jnp.float32)
    row_loss = lse - jnp.sum(zp * hit, axis=1)
    grad_p = (jnp.exp(zp - lse[:, None]) - hit).astype(jnp.bfloat16)
    grad_q = (weight * jnp.exp(zq - lse[:, None])).astype(jnp.bfloat16)

    mid = n_pass // 2
    bits = [("wide", 1 << (b + 1), swap_pairs(n_dev, 1 << (b + 1))) for b in range(n_chip.bit_length() - 1)]
    dims = [("x", bits[0][2])] + [("z%d" % i, b[2]) for i, b in enumerate(bits[1:])]
    names = (["y"] if parts == 2 else []) + [d[0] for d in reversed(dims)]
    pairs_of = dict(dims)

    def reduced(columns, orders):
        def terms(grads):
            return lax.dot_general(
                grads, columns, (((0,), (0,)), ((), ())), preferred_element_type=jnp.float32
            )

        got = lax.ppermute(terms(grad_p[:, mid:]), "wide", swap)
        sums = (terms(grad_p[:, :mid]) + got).reshape((2,) * len(names) + (sub, columns.shape[1]))
        left = list(names)
        for name in orders:
            at = left.index(name)
            sent = lax.index_in_dim(sums, 1, at, keepdims=False).astype(jnp.bfloat16)
            if name == "y":
                got = lax.ppermute(sent, "dp", across)
            else:
                got = lax.ppermute(sent, "wide", pairs_of[name])
            sums = lax.index_in_dim(sums, 0, at, keepdims=False) + got.astype(jnp.float32)
            left.pop(at)
        return sums

    zs = [d[0] for d in dims[1:]]
    if parts == 2:
        orders = (["y", "x"] + zs, ["x", "y"] + zs)
    else:
        orders = (["x"] + zs, zs + ["x"])
    cut = width // 2
    own = jnp.concatenate(
        [reduced(queries[:, :cut], orders[0]), reduced(queries[:, cut:], orders[1])], 1
    )
    if parts == 2:
        own = own * scale
        got = lax.ppermute(own, "dp", across)
        low, high = jnp.where(replica == 0, own, got), jnp.where(replica == 0, got, own)
        passage_grad = jnp.concatenate([low, high], 0)
    else:
        passage_grad = lax.psum(own, "dp") * scale

    qgrad = jnp.dot(grad_p, pieces, preferred_element_type=jnp.float32) + jnp.dot(
        grad_q, pool_s, preferred_element_type=jnp.float32
    )
    query_grad = (qgrad * scale).astype(jnp.bfloat16)
    return (row_loss, query_grad, passage_grad)


def solution(mesh):
    placed = (
        P(("wide", "dp"), None),
        P(("wide", "dp"), None),
        P("wide", None),
        P("wide", None),
        P("wide", None),
        P("dp"),
        P(("wide", "dp")),
        P(("wide", "dp"), None),
    )
    return jax.shard_map(
        body,
        mesh=mesh,
        in_specs=placed,
        out_specs=(P(("wide", "dp")), P(("wide", "dp"), None), P("wide", None)),
        check_vma=False,
    )
```

```python
import functools
import math

import jax
import jax.numpy as jnp
from jax import lax
from jax.experimental import pallas as pl
from jax.experimental.pallas import tpu as pltpu
from jax.sharding import PartitionSpec as P

STEP = 32
VMEM_LIMIT = 24 * 2**20


def ring_order(n_chip):
    nz = n_chip // 2
    return [2 * z for z in range(nz)] + [2 * z + 1 for z in reversed(range(nz))]


def ring_pairs(n_chip):
    order = ring_order(n_chip)
    pairs = []
    for i, chip in enumerate(order):
        pairs.append((2 * chip, 2 * order[(i + 1) % n_chip]))
        pairs.append((2 * chip + 1, 2 * order[(i - 1) % n_chip] + 1))
    return pairs


def swap_pairs(n, bit):
    return [(i, i ^ bit) for i in range(n)]


def rows_at(x, tile, count):
    return lax.dynamic_slice_in_dim(x, tile * 8, count, 0)


def put_rows(x, rows, tile):
    return lax.dynamic_update_slice_in_dim(x, rows, tile * 8, 0)


def gather_rows(bank_s, bank_t, passages, owner, index, core, waiting):
    n_dev = lax.axis_size("wide")
    n_chip = n_dev // 2
    pool, width = bank_s.shape
    n_chunk = pool // STEP
    n_cut = max(1, 3 * n_chunk // 8)
    n_own = n_chunk - n_cut
    rounds = max(n_cut + n_chip - 2, n_own + n_chip // 2 - 1)
    block = passages.shape[0]
    sub = block // 2
    chip = index // 2

    def place(c):
        return jnp.where(c % 2 == 0, c // 2, n_chip - 1 - c // 2)

    def chip_at(p):
        return jnp.where(p < n_chip // 2, 2 * p, 2 * (n_chip - 1 - p) + 1)

    here = place(chip)
    turn = 1 - 2 * core
    away = here - place(owner // 2)
    distance = (turn * away + n_chip) % n_chip
    distance_other = (n_chip - turn * away) % n_chip
    own_chip = owner // 2 == chip
    own_core = owner == index
    swap = swap_pairs(n_dev, 1)
    pairs = ring_pairs(n_chip)

    banks = [bank_s, bank_t]
    swapped = [None, lax.ppermute(bank_t, "wide", swap)]
    swapped[0] = lax.ppermute(bank_s, "wide", swap)

    def tile_of(side, slot):
        return jnp.where(side == 0, slot, n_chunk - 1 - slot) * (STEP // 8)

    def own_rows(i, j):
        at = tile_of(core, j)
        return jnp.where(own_core, rows_at(banks[i], at, STEP), rows_at(swapped[i], at, STEP))

    pools = [jnp.zeros_like(bank_s), jnp.zeros_like(bank_t)]
    rows = put_rows(jnp.zeros((n_chip * block, width), passages.dtype), passages, 0)
    moving = [own_rows(i, 0) for i in range(2)]
    riding = [passages[:sub], passages[sub:]]
    arrived = [[], []]

    def keep(i, t, sent):
        other = lax.ppermute(sent, "wide", swap)
        for side, away, piece in ((core, distance, sent), (1 - core, distance_other, other)):
            slot = t - away
            take = (slot >= 0) & (slot < n_own)
            at = tile_of(side, jnp.clip(slot, 0, n_own - 1))
            pools[i] = put_rows(pools[i], jnp.where(take, piece, rows_at(pools[i], at, STEP)), at)

    for t in range(rounds):
        for i in (1, 0):
            sent = jnp.concatenate([moving[i], riding[i]], 0) if t < n_chip - 1 else moving[i]
            before = t - 1 - i
            if before >= 0:
                sent, arrived[1 - i][before] = lax.optimization_barrier((sent, arrived[1 - i][before]))
            if t == 0:
                (banks[i], swapped[i]), sent = lax.optimization_barrier(((banks[i], swapped[i]), sent))
                full = jnp.where(own_core, banks[i], swapped[i])
                banks[i], swapped[i] = full, full
            got = lax.ppermute(sent, "wide", pairs)
            arrived[i].append(got)
            keep(i, t, sent[:STEP])
            if i == 0 and t == 3:
                waiting, got = lax.optimization_barrier((waiting, got))
            if t < n_chip - 1:
                riding[i] = got[STEP:]
                got = got[:STEP]
                origin = chip_at((here - turn * (t + 1) + n_chip) % n_chip)
                rows = put_rows(rows, riding[i], (origin ^ chip) * (block // 8) + i * (sub // 8))
            moving[i] = got
            if t + 1 < n_own:
                moving[i] = jnp.where(own_chip, own_rows(i, t + 1), got)
    for i in (1, 0):
        keep(i, rounds, moving[i])
    return pools[0], pools[1], rows, waiting


def dot_t(a, b):
    return lax.dot_general(a, b, (((1,), (1,)), ((), ())), preferred_element_type=jnp.float32)


def tail_kernel(scale, n_rows, *refs):
    pass_refs, refs = refs[:n_rows], refs[n_rows:]
    q, tq, pool_s, pool_t, mask, column = refs[:6]
    gp, gq, loss, pieces = refs[6:]
    n_query, width = q.shape
    first = 0
    for ref in pass_refs:
        pieces[first : first + ref.shape[0], :] = ref[...]
        first += ref.shape[0]
    block = min(256, n_query)

    @pl.loop(0, n_query // block)
    def _(b):
        at = pl.ds(pl.multiple_of(b * block, block), block)
        p = dot_t(q[at, :], pieces[...]) * scale
        z = dot_t(q[at, :], pool_s[...]) * scale
        tt = dot_t(tq[at, :], pool_t[...]) * scale
        weight = mask[at, :].astype(jnp.float32) * jax.nn.sigmoid(-tt)
        top = jnp.maximum(jnp.max(p, axis=1, keepdims=True), jnp.max(z, axis=1, keepdims=True))
        total = jnp.sum(jnp.exp(p - top), axis=1, keepdims=True) + jnp.sum(
            weight * jnp.exp(z - top), axis=1, keepdims=True
        )
        lse = top + jnp.log(total)
        hit = (lax.broadcasted_iota(jnp.int32, p.shape, 1) == column[at, :]).astype(jnp.float32)
        loss[at, :] = lse - jnp.sum(p * hit, axis=1, keepdims=True)
        gp[at, :] = (jnp.exp(p - lse) - hit).astype(jnp.bfloat16)
        gq[at, :] = (weight * jnp.exp(z - lse)).astype(jnp.bfloat16)


def tail(scale, pass_parts, queries, teacher, pool_s, pool_t, mask, column):
    n_query, width = queries.shape
    n_pass = sum(p.shape[0] for p in pass_parts)
    pool = pool_s.shape[0]
    bf16, f32 = jnp.bfloat16, jnp.float32
    arrays = [*pass_parts, queries, teacher, pool_s, pool_t, mask, column]
    vmem = pl.BlockSpec(memory_space=pltpu.VMEM)
    return pl.pallas_call(
        functools.partial(tail_kernel, scale, len(pass_parts)),
        out_shape=[
            jax.ShapeDtypeStruct((n_query, n_pass), bf16),
            jax.ShapeDtypeStruct((n_query, pool), bf16),
            jax.ShapeDtypeStruct((n_query, 1), f32),
            jax.ShapeDtypeStruct((n_pass, width), bf16),
        ],
        in_specs=[vmem] * len(arrays),
        out_specs=[vmem] * 4,
        compiler_params=pltpu.CompilerParams(vmem_limit_bytes=VMEM_LIMIT),
        cost_estimate=pl.CostEstimate(
            flops=2 * n_query * width * (n_pass + 2 * pool),
            bytes_accessed=4 * width * (n_query + 2 * n_pass + pool),
            transcendentals=0,
        ),
        name="scores",
    )(*arrays)


def body(
    queries, teacher_queries, passages, bank_student, bank_teacher, owner, positives, keep_mask
):
    n_dev = lax.axis_size("wide")
    n_chip = n_dev // 2
    n_dp = lax.axis_size("dp")
    index = lax.axis_index("wide")
    replica = lax.axis_index("dp")
    core = index % 2
    chip = index // 2
    block, width = passages.shape
    scale = 2.0 / math.sqrt(width)
    n_pass = block * n_dev
    swap = swap_pairs(n_dev, 1)
    across = [(0, 1), (1, 0)]
    pool_s, pool_t, rows, keep_mask = gather_rows(
        bank_student, bank_teacher, passages, owner[0], index, core, keep_mask
    )
    pass_parts = [rows, lax.ppermute(rows, "wide", swap)]
    chip_of = (positives // (2 * block)) ^ chip
    core_of = ((positives // block) % 2) ^ core
    column = (core_of * n_chip + chip_of) * block + positives % block
    grad_p, grad_q, row_loss, pieces = tail(
        scale, pass_parts, queries, teacher_queries, pool_s, pool_t, keep_mask, column[:, None]
    )

    chip_bits = ["x"] + ["z%d" % b for b in range(n_chip.bit_length() - 2)]
    pairs_of = {name: swap_pairs(n_dev, 2 << b) for b, name in enumerate(chip_bits)}
    first_sent = []

    def reduced(columns, order):
        def terms(grads):
            return lax.dot_general(
                grads, columns, (((0,), (0,)), ((), ())), preferred_element_type=jnp.float32
            )

        got = lax.ppermute(terms(grad_p[:, mid:]), "wide", swap)
        sums = (terms(grad_p[:, :mid]) + got).reshape(
            (2,) * len(chip_bits) + (block, columns.shape[1])
        )
        left = chip_bits[::-1]
        for name in order:
            at = left.index(name)
            sent = lax.index_in_dim(sums, 1, at, keepdims=False).astype(jnp.bfloat16)
            first_sent.append(sent)
            got = lax.ppermute(sent, "wide", pairs_of[name])
            sums = lax.index_in_dim(sums, 0, at, keepdims=False) + got.astype(jnp.float32)
            left.pop(at)
        if n_dp != 2:
            return lax.psum(sums, "dp") * scale
        return (sums + lax.ppermute(sums, "dp", across)) * scale

    mid, half = n_pass // 2, width // 2
    zs = chip_bits[1:]
    passage_grad = jnp.concatenate(
        [
            reduced(queries[:, :half], ["x"] + zs),
            reduced(queries[:, half:], zs[:1] + ["x"] + zs[1:]),
        ],
        1,
    )

    (late_p, grad_q), _ = lax.optimization_barrier(((grad_p, grad_q), first_sent[0]))
    qgrad = jnp.dot(late_p, pieces, preferred_element_type=jnp.float32) + jnp.dot(
        grad_q, pool_s, preferred_element_type=jnp.float32
    )
    query_grad = (qgrad * scale).astype(jnp.bfloat16)
    return (row_loss[:, 0], query_grad, passage_grad)


def solution(mesh):
    placed = (
        P(("wide", "dp"), None),
        P(("wide", "dp"), None),
        P("wide", None),
        P("wide", None),
        P("wide", None),
        P("dp"),
        P(("wide", "dp")),
        P(("wide", "dp"), None),
    )
    return jax.shard_map(
        body,
        mesh=mesh,
        in_specs=placed,
        out_specs=(P(("wide", "dp")), P(("wide", "dp"), None), P("wide", None)),
        check_vma=False,
    )
```

```python
import functools
import math

import jax
import jax.numpy as jnp
from jax import lax
from jax.experimental import pallas as pl
from jax.experimental.pallas import tpu as pltpu
from jax.sharding import PartitionSpec as P

STEP = 32
VMEM_LIMIT = 24 * 2**20


def ring_order(n_chip):
    nz = n_chip // 2
    return [2 * z for z in range(nz)] + [2 * z + 1 for z in reversed(range(nz))]


def ring_pairs(n_chip):
    order = ring_order(n_chip)
    pairs = []
    for i, chip in enumerate(order):
        pairs.append((2 * chip, 2 * order[(i + 1) % n_chip]))
        pairs.append((2 * chip + 1, 2 * order[(i - 1) % n_chip] + 1))
    return pairs


def swap_pairs(n, bit):
    return [(i, i ^ bit) for i in range(n)]


def rows_at(x, tile, count):
    return lax.dynamic_slice_in_dim(x, tile * 8, count, 0)


def put_rows(x, rows, tile):
    return lax.dynamic_update_slice_in_dim(x, rows, tile * 8, 0)


def gather_rows(bank_s, bank_t, passages, owner, index, core):
    n_dev = lax.axis_size("wide")
    n_chip = n_dev // 2
    pool, width = bank_s.shape
    n_chunk = pool // STEP
    n_cut = max(1, 3 * n_chunk // 8)
    n_own = n_chunk - n_cut
    rounds = max(n_cut + n_chip - 2, n_own + n_chip // 2 - 1)
    block = passages.shape[0]
    sub = block // 2
    chip = index // 2

    def place(c):
        return jnp.where(c % 2 == 0, c // 2, n_chip - 1 - c // 2)

    def chip_at(p):
        return jnp.where(p < n_chip // 2, 2 * p, 2 * (n_chip - 1 - p) + 1)

    here = place(chip)
    turn = 1 - 2 * core
    away = here - place(owner // 2)
    distance = (turn * away + n_chip) % n_chip
    distance_other = (n_chip - turn * away) % n_chip
    own_chip = owner // 2 == chip
    own_core = owner == index
    swap = swap_pairs(n_dev, 1)
    pairs = ring_pairs(n_chip)

    banks = [bank_s, bank_t]
    swapped = [None, lax.ppermute(bank_t, "wide", swap)]
    swapped[0] = lax.ppermute(bank_s, "wide", swap)

    def tile_of(side, slot):
        return jnp.where(side == 0, slot, n_chunk - 1 - slot) * (STEP // 8)

    def own_rows(i, j):
        at = tile_of(core, j)
        return jnp.where(own_core, rows_at(banks[i], at, STEP), rows_at(swapped[i], at, STEP))

    pools = [jnp.zeros_like(bank_s), jnp.zeros_like(bank_t)]
    rows = put_rows(jnp.zeros((n_chip * block, width), passages.dtype), passages, 0)
    moving = [own_rows(i, 0) for i in range(2)]
    riding = [passages[:sub], passages[sub:]]
    arrived = [[], []]

    def keep(i, t, sent):
        other = lax.ppermute(sent, "wide", swap)
        for side, away, piece in ((core, distance, sent), (1 - core, distance_other, other)):
            slot = t - away
            take = (slot >= 0) & (slot < n_own)
            at = tile_of(side, jnp.clip(slot, 0, n_own - 1))
            pools[i] = put_rows(pools[i], jnp.where(take, piece, rows_at(pools[i], at, STEP)), at)

    for t in range(rounds):
        for i in (1, 0):
            sent = jnp.concatenate([moving[i], riding[i]], 0) if t < n_chip - 1 else moving[i]
            before = t - 1 - i
            if before >= 0:
                sent, arrived[1 - i][before] = lax.optimization_barrier((sent, arrived[1 - i][before]))
            if t == 0:
                (banks[i], swapped[i]), sent = lax.optimization_barrier(((banks[i], swapped[i]), sent))
                full = jnp.where(own_core, banks[i], swapped[i])
                banks[i], swapped[i] = full, full
            got = lax.ppermute(sent, "wide", pairs)
            arrived[i].append(got)
            keep(i, t, sent[:STEP])
            if t < n_chip - 1:
                riding[i] = got[STEP:]
                got = got[:STEP]
                origin = chip_at((here - turn * (t + 1) + n_chip) % n_chip)
                rows = put_rows(rows, riding[i], (origin ^ chip) * (block // 8) + i * (sub // 8))
            moving[i] = got
            if t + 1 < n_own:
                moving[i] = jnp.where(own_chip, own_rows(i, t + 1), got)
    for i in (1, 0):
        keep(i, rounds, moving[i])
    return pools[0], pools[1], rows


def dot_t(a, b):
    return lax.dot_general(a, b, (((1,), (1,)), ((), ())), preferred_element_type=jnp.float32)


def tail_kernel(scale, n_rows, *refs):
    pass_refs, refs = refs[:n_rows], refs[n_rows:]
    q, tq, pool_s, pool_t, mask, column = refs[:6]
    gp, gq, loss, pieces = refs[6:]
    n_query, width = q.shape
    first = 0
    for ref in pass_refs:
        pieces[first : first + ref.shape[0], :] = ref[...]
        first += ref.shape[0]
    block = min(256, n_query)

    @pl.loop(0, n_query // block)
    def _(b):
        at = pl.ds(pl.multiple_of(b * block, block), block)
        p = dot_t(q[at, :], pieces[...]) * scale
        z = dot_t(q[at, :], pool_s[...]) * scale
        tt = dot_t(tq[at, :], pool_t[...]) * scale
        weight = mask[at, :].astype(jnp.float32) * jax.nn.sigmoid(-tt)
        top = jnp.maximum(jnp.max(p, axis=1, keepdims=True), jnp.max(z, axis=1, keepdims=True))
        total = jnp.sum(jnp.exp(p - top), axis=1, keepdims=True) + jnp.sum(
            weight * jnp.exp(z - top), axis=1, keepdims=True
        )
        lse = top + jnp.log(total)
        hit = (lax.broadcasted_iota(jnp.int32, p.shape, 1) == column[at, :]).astype(jnp.float32)
        loss[at, :] = lse - jnp.sum(p * hit, axis=1, keepdims=True)
        gp[at, :] = (jnp.exp(p - lse) - hit).astype(jnp.bfloat16)
        gq[at, :] = (weight * jnp.exp(z - lse)).astype(jnp.bfloat16)


def tail(scale, pass_parts, queries, teacher, pool_s, pool_t, mask, column):
    n_query, width = queries.shape
    n_pass = sum(p.shape[0] for p in pass_parts)
    pool = pool_s.shape[0]
    bf16, f32 = jnp.bfloat16, jnp.float32
    arrays = [*pass_parts, queries, teacher, pool_s, pool_t, mask, column]
    vmem = pl.BlockSpec(memory_space=pltpu.VMEM)
    return pl.pallas_call(
        functools.partial(tail_kernel, scale, len(pass_parts)),
        out_shape=[
            jax.ShapeDtypeStruct((n_query, n_pass), bf16),
            jax.ShapeDtypeStruct((n_query, pool), bf16),
            jax.ShapeDtypeStruct((n_query, 1), f32),
            jax.ShapeDtypeStruct((n_pass, width), bf16),
        ],
        in_specs=[vmem] * len(arrays),
        out_specs=[vmem] * 4,
        compiler_params=pltpu.CompilerParams(vmem_limit_bytes=VMEM_LIMIT),
        cost_estimate=pl.CostEstimate(
            flops=2 * n_query * width * (n_pass + 2 * pool),
            bytes_accessed=4 * width * (n_query + 2 * n_pass + pool),
            transcendentals=0,
        ),
        name="scores",
    )(*arrays)


def body(
    queries, teacher_queries, passages, bank_student, bank_teacher, owner, positives, keep_mask
):
    n_dev = lax.axis_size("wide")
    n_chip = n_dev // 2
    n_dp = lax.axis_size("dp")
    index = lax.axis_index("wide")
    replica = lax.axis_index("dp")
    core = index % 2
    chip = index // 2
    block, width = passages.shape
    scale = 2.0 / math.sqrt(width)
    n_pass = block * n_dev
    swap = swap_pairs(n_dev, 1)
    across = [(0, 1), (1, 0)]
    pool_s, pool_t, rows = gather_rows(bank_student, bank_teacher, passages, owner[0], index, core)
    pass_parts = [rows, lax.ppermute(rows, "wide", swap)]
    chip_of = (positives // (2 * block)) ^ chip
    core_of = ((positives // block) % 2) ^ core
    column = (core_of * n_chip + chip_of) * block + positives % block
    grad_p, grad_q, row_loss, pieces = tail(
        scale, pass_parts, queries, teacher_queries, pool_s, pool_t, keep_mask, column[:, None]
    )

    chip_bits = ["x"] + ["z%d" % b for b in range(n_chip.bit_length() - 2)]
    pairs_of = {name: swap_pairs(n_dev, 2 << b) for b, name in enumerate(chip_bits)}
    zs = chip_bits[1:]
    orders = (["x"] + zs, zs[:1] + ["x"] + zs[1:])
    lefts = [chip_bits[::-1], chip_bits[::-1]]
    sums = []
    sent = [None, None]
    mid, half = n_pass // 2, width // 2
    for h in range(2):
        columns = queries[:, h * half : (h + 1) * half]

        def terms(grads):
            return lax.dot_general(
                grads, columns, (((0,), (0,)), ((), ())), preferred_element_type=jnp.float32
            )

        got = lax.ppermute(terms(grad_p[:, mid:]), "wide", swap)
        sums.append((terms(grad_p[:, :mid]) + got).reshape((2,) * len(chip_bits) + (block, half)))
    for step in range(len(chip_bits)):
        for h in range(2):
            at = lefts[h].index(orders[h][step])
            sent[h] = lax.index_in_dim(sums[h], 1, at, keepdims=False).astype(jnp.bfloat16)
            sums[h] = lax.index_in_dim(sums[h], 0, at, keepdims=False)
            lefts[h].pop(at)
            if h == 1:
                sent[1], _ = lax.optimization_barrier((sent[1], sent[0]))
            got = lax.ppermute(sent[h], "wide", pairs_of[orders[h][step]])
            sums[h] = sums[h] + got.astype(jnp.float32)
        if step == 0:
            (late_p, grad_q, row_loss), _ = lax.optimization_barrier(((grad_p, grad_q, row_loss), sent[1]))
    if n_dp == 2:
        sums[1], _ = lax.optimization_barrier((sums[1], sums[0]))
        sums = [x + lax.ppermute(x, "dp", across) for x in sums]
    else:
        sums = [lax.psum(x, "dp") for x in sums]
    passage_grad = jnp.concatenate(sums, 1) * scale

    qgrad = jnp.dot(late_p, pieces, preferred_element_type=jnp.float32) + jnp.dot(
        grad_q, pool_s, preferred_element_type=jnp.float32
    )
    query_grad = (qgrad * scale).astype(jnp.bfloat16)
    return (row_loss[:, 0], query_grad, passage_grad)


def solution(mesh):
    placed = (
        P(("wide", "dp"), None),
        P(("wide", "dp"), None),
        P("wide", None),
        P("wide", None),
        P("wide", None),
        P("dp"),
        P(("wide", "dp")),
        P(("wide", "dp"), None),
    )
    return jax.shard_map(
        body,
        mesh=mesh,
        in_specs=placed,
        out_specs=(P(("wide", "dp")), P(("wide", "dp"), None), P("wide", None)),
        check_vma=False,
    )
```

```python
import functools
import math

import jax
import jax.numpy as jnp
from jax import lax
from jax.experimental import pallas as pl
from jax.experimental.pallas import tpu as pltpu
from jax.sharding import PartitionSpec as P

STEP = 32
VMEM_LIMIT = 24 * 2**20


def ring_order(n_chip):
    nz = n_chip // 2
    return [2 * z for z in range(nz)] + [2 * z + 1 for z in reversed(range(nz))]


def ring_pairs(n_chip):
    order = ring_order(n_chip)
    pairs = []
    for i, chip in enumerate(order):
        pairs.append((2 * chip, 2 * order[(i + 1) % n_chip]))
        pairs.append((2 * chip + 1, 2 * order[(i - 1) % n_chip] + 1))
    return pairs


def swap_pairs(n, bit):
    return [(i, i ^ bit) for i in range(n)]


def rows_at(x, tile, count):
    return lax.dynamic_slice_in_dim(x, tile * 8, count, 0)


def put_rows(x, rows, tile):
    return lax.dynamic_update_slice_in_dim(x, rows, tile * 8, 0)


def gather_rows(bank_s, bank_t, passages, owner, index, core):
    n_dev = lax.axis_size("wide")
    n_chip = n_dev // 2
    pool, width = bank_s.shape
    n_chunk = pool // STEP
    rounds = max((n_chunk + n_chip - 1) // 2, n_chip - 1)
    block = passages.shape[0]
    sub = block // 2
    chip = index // 2

    def place(c):
        return jnp.where(c % 2 == 0, c // 2, n_chip - 1 - c // 2)

    def chip_at(p):
        return jnp.where(p < n_chip // 2, 2 * p, 2 * (n_chip - 1 - p) + 1)

    here = place(chip)
    turn = 1 - 2 * core
    away = here - place(owner // 2)
    distance = (turn * away + n_chip) % n_chip
    distance_other = (n_chip - turn * away) % n_chip
    own_chip = owner // 2 == chip
    own_core = owner == index
    swap = swap_pairs(n_dev, 1)
    pairs = ring_pairs(n_chip)

    banks = [bank_s, bank_t]
    swapped = [None, lax.ppermute(bank_t, "wide", swap)]
    swapped[0] = lax.ppermute(bank_s, "wide", swap)

    def tile_of(side, slot):
        return jnp.where(side == 0, slot, n_chunk - 1 - slot) * (STEP // 8)

    def own_rows(i, j):
        at = tile_of(core, j)
        return jnp.where(own_core, rows_at(banks[i], at, STEP), rows_at(swapped[i], at, STEP))

    pools = [jnp.zeros_like(bank_s), jnp.zeros_like(bank_t)]
    rows = put_rows(jnp.zeros((n_chip * block, width), passages.dtype), passages, 0)
    moving = [own_rows(i, 0) for i in range(2)]
    riding = [passages[:sub], passages[sub:]]
    arrived = [[], []]

    def keep(i, t, sent):
        other = lax.ppermute(sent, "wide", swap)
        for side, away, piece in ((core, distance, sent), (1 - core, distance_other, other)):
            slot = t - away
            take = (slot >= 0) & (slot < n_chunk)
            at = tile_of(side, jnp.clip(slot, 0, n_chunk - 1))
            pools[i] = put_rows(pools[i], jnp.where(take, piece, rows_at(pools[i], at, STEP)), at)

    for t in range(rounds):
        for i in (1, 0):
            sent = jnp.concatenate([moving[i], riding[i]], 0) if t < n_chip - 1 else moving[i]
            before = t - 1 - i
            if before >= 0:
                sent, arrived[1 - i][before] = lax.optimization_barrier((sent, arrived[1 - i][before]))
            if t == 0:
                (banks[i], swapped[i]), sent = lax.optimization_barrier(((banks[i], swapped[i]), sent))
                full = jnp.where(own_core, banks[i], swapped[i])
                banks[i], swapped[i] = full, full
            got = lax.ppermute(sent, "wide", pairs)
            arrived[i].append(got)
            keep(i, t, sent[:STEP])
            if t < n_chip - 1:
                riding[i] = got[STEP:]
                got = got[:STEP]
                origin = chip_at((here - turn * (t + 1) + n_chip) % n_chip)
                rows = put_rows(rows, riding[i], (origin ^ chip) * (block // 8) + i * (sub // 8))
            moving[i] = got
            if t + 1 < n_chunk:
                moving[i] = jnp.where(own_chip, own_rows(i, t + 1), got)
    for i in (1, 0):
        keep(i, rounds, moving[i])
    return pools[0], pools[1], rows


def dot_t(a, b):
    return lax.dot_general(a, b, (((1,), (1,)), ((), ())), preferred_element_type=jnp.float32)


def tail_kernel(scale, n_rows, *refs):
    pass_refs, refs = refs[:n_rows], refs[n_rows:]
    q, tq, pool_s, pool_t, mask, column = refs[:6]
    gp, gq, loss, pieces = refs[6:]
    n_query, width = q.shape
    first = 0
    for ref in pass_refs:
        pieces[first : first + ref.shape[0], :] = ref[...]
        first += ref.shape[0]
    block = min(256, n_query)

    @pl.loop(0, n_query // block)
    def _(b):
        at = pl.ds(pl.multiple_of(b * block, block), block)
        p = dot_t(q[at, :], pieces[...]) * scale
        z = dot_t(q[at, :], pool_s[...]) * scale
        tt = dot_t(tq[at, :], pool_t[...]) * scale
        weight = mask[at, :].astype(jnp.float32) * jax.nn.sigmoid(-tt)
        top = jnp.maximum(jnp.max(p, axis=1, keepdims=True), jnp.max(z, axis=1, keepdims=True))
        total = jnp.sum(jnp.exp(p - top), axis=1, keepdims=True) + jnp.sum(
            weight * jnp.exp(z - top), axis=1, keepdims=True
        )
        lse = top + jnp.log(total)
        hit = (lax.broadcasted_iota(jnp.int32, p.shape, 1) == column[at, :]).astype(jnp.float32)
        loss[at, :] = lse - jnp.sum(p * hit, axis=1, keepdims=True)
        gp[at, :] = (jnp.exp(p - lse) - hit).astype(jnp.bfloat16)
        gq[at, :] = (weight * jnp.exp(z - lse)).astype(jnp.bfloat16)


def tail(scale, pass_parts, queries, teacher, pool_s, pool_t, mask, column):
    n_query, width = queries.shape
    n_pass = sum(p.shape[0] for p in pass_parts)
    pool = pool_s.shape[0]
    bf16, f32 = jnp.bfloat16, jnp.float32
    arrays = [*pass_parts, queries, teacher, pool_s, pool_t, mask, column]
    vmem = pl.BlockSpec(memory_space=pltpu.VMEM)
    return pl.pallas_call(
        functools.partial(tail_kernel, scale, len(pass_parts)),
        out_shape=[
            jax.ShapeDtypeStruct((n_query, n_pass), bf16),
            jax.ShapeDtypeStruct((n_query, pool), bf16),
            jax.ShapeDtypeStruct((n_query, 1), f32),
            jax.ShapeDtypeStruct((n_pass, width), bf16),
        ],
        in_specs=[vmem] * len(arrays),
        out_specs=[vmem] * 4,
        compiler_params=pltpu.CompilerParams(vmem_limit_bytes=VMEM_LIMIT),
        cost_estimate=pl.CostEstimate(
            flops=2 * n_query * width * (n_pass + 2 * pool),
            bytes_accessed=4 * width * (n_query + 2 * n_pass + pool),
            transcendentals=0,
        ),
        name="scores",
    )(*arrays)


def body(
    queries, teacher_queries, passages, bank_student, bank_teacher, owner, positives, keep_mask
):
    n_dev = lax.axis_size("wide")
    n_chip = n_dev // 2
    n_dp = lax.axis_size("dp")
    index = lax.axis_index("wide")
    replica = lax.axis_index("dp")
    core = index % 2
    chip = index // 2
    block, width = passages.shape
    scale = 2.0 / math.sqrt(width)
    n_pass = block * n_dev
    swap = swap_pairs(n_dev, 1)
    across = [(0, 1), (1, 0)]
    pool_s, pool_t, rows = gather_rows(bank_student, bank_teacher, passages, owner[0], index, core)
    pass_parts = [rows, lax.ppermute(rows, "wide", swap)]
    chip_of = (positives // (2 * block)) ^ chip
    core_of = ((positives // block) % 2) ^ core
    column = (core_of * n_chip + chip_of) * block + positives % block
    grad_p, grad_q, row_loss, pieces = tail(
        scale, pass_parts, queries, teacher_queries, pool_s, pool_t, keep_mask, column[:, None]
    )

    chip_bits = ["x"] + ["z%d" % b for b in range(n_chip.bit_length() - 2)]
    pairs_of = {name: swap_pairs(n_dev, 2 << b) for b, name in enumerate(chip_bits)}
    zs = chip_bits[1:]
    orders = (["x"] + zs, zs[:1] + ["x"] + zs[1:])
    lefts = [chip_bits[::-1], chip_bits[::-1]]
    sums = []
    sent = [None, None]
    mid, half = n_pass // 2, width // 2
    for h in range(2):
        columns = queries[:, h * half : (h + 1) * half]

        def terms(grads):
            return lax.dot_general(
                grads, columns, (((0,), (0,)), ((), ())), preferred_element_type=jnp.float32
            )

        got = lax.ppermute(terms(grad_p[:, mid:]).astype(jnp.bfloat16), "wide", swap)
        sums.append((terms(grad_p[:, :mid]) + got.astype(jnp.float32)).reshape((2,) * len(chip_bits) + (block, half)))
    pending = None
    for step in range(len(chip_bits)):
        for h in range(2):
            if h == 1 and step:
                pending, _ = lax.optimization_barrier((pending, sent[0]))
                sums[1] = sums[1] + pending.astype(jnp.float32)
            at = lefts[h].index(orders[h][step])
            sent[h] = lax.index_in_dim(sums[h], 1, at, keepdims=False).astype(jnp.bfloat16)
            sums[h] = lax.index_in_dim(sums[h], 0, at, keepdims=False)
            lefts[h].pop(at)
            if h == 1 and step == 0:
                sent[1], _ = lax.optimization_barrier((sent[1], sent[0]))
            got = lax.ppermute(sent[h], "wide", pairs_of[orders[h][step]])
            if h == 0:
                sums[0] = sums[0] + got.astype(jnp.float32)
            else:
                pending = got
        if step == 0:
            (late_p, grad_q, row_loss), _ = lax.optimization_barrier(((grad_p, grad_q, row_loss), sent[1]))
    pending, _ = lax.optimization_barrier((pending, sums[0]))
    sums[1] = sums[1] + pending.astype(jnp.float32)
    if n_dp == 2:
        sums = [x + lax.ppermute(x, "dp", across) for x in sums]
    else:
        sums = [lax.psum(x, "dp") for x in sums]
    passage_grad = jnp.concatenate(sums, 1) * scale

    qgrad = jnp.dot(late_p, pieces, preferred_element_type=jnp.float32) + jnp.dot(
        grad_q, pool_s, preferred_element_type=jnp.float32
    )
    query_grad = (qgrad * scale).astype(jnp.bfloat16)
    return (row_loss[:, 0], query_grad, passage_grad)


def solution(mesh):
    placed = (
        P(("wide", "dp"), None),
        P(("wide", "dp"), None),
        P("wide", None),
        P("wide", None),
        P("wide", None),
        P("dp"),
        P(("wide", "dp")),
        P(("wide", "dp"), None),
    )
    return jax.shard_map(
        body,
        mesh=mesh,
        in_specs=placed,
        out_specs=(P(("wide", "dp")), P(("wide", "dp"), None), P("wide", None)),
        check_vma=False,
    )
```

```python
import functools
import math

import jax
import jax.numpy as jnp
from jax import lax
from jax.experimental import pallas as pl
from jax.experimental.pallas import tpu as pltpu
from jax.sharding import PartitionSpec as P

STEP = 32
VMEM_LIMIT = 24 * 2**20


def ring_order(n_chip):
    nz = n_chip // 2
    return [2 * z for z in range(nz)] + [2 * z + 1 for z in reversed(range(nz))]


def ring_pairs(n_chip):
    order = ring_order(n_chip)
    pairs = []
    for i, chip in enumerate(order):
        pairs.append((2 * chip, 2 * order[(i + 1) % n_chip]))
        pairs.append((2 * chip + 1, 2 * order[(i - 1) % n_chip] + 1))
    return pairs


def swap_pairs(n, bit):
    return [(i, i ^ bit) for i in range(n)]


def rows_at(x, tile, count):
    return lax.dynamic_slice_in_dim(x, tile * 8, count, 0)


def put_rows(x, rows, tile):
    return lax.dynamic_update_slice_in_dim(x, rows, tile * 8, 0)


def first_kernel(side_ref, bank_s, bank_t, *refs):
    outs = refs
    pool = bank_s.shape[0]
    for n, out in enumerate(outs):
        side = side_ref[0] if n < 2 else 1 - side_ref[0]
        at = pl.multiple_of(side * (pool - 2 * STEP), STEP)
        out[...] = (bank_s, bank_t)[n % 2][pl.ds(at, 2 * STEP), :]


def first_chunks(bank_s, bank_t, core):
    chunk = jax.ShapeDtypeStruct((2 * STEP, bank_s.shape[1]), bank_s.dtype)
    return pl.pallas_call(
        first_kernel,
        out_shape=[chunk] * 4,
        in_specs=[pl.BlockSpec(memory_space=pltpu.SMEM)] + [pl.BlockSpec(memory_space=pltpu.VMEM)] * 2,
        out_specs=[pl.BlockSpec(memory_space=pltpu.VMEM)] * 4,
        compiler_params=pltpu.CompilerParams(vmem_limit_bytes=VMEM_LIMIT),
        name="first_chunks",
    )(core.astype(jnp.int32)[None], bank_s, bank_t)


def gather_rows(bank_s, bank_t, passages, owner, index, core):
    n_dev = lax.axis_size("wide")
    n_chip = n_dev // 2
    pool, width = bank_s.shape
    n_chunk = pool // STEP
    rounds = max((n_chunk + n_chip - 1) // 2, n_chip - 1)
    block = passages.shape[0]
    sub = block // 2
    chip = index // 2

    def place(c):
        return jnp.where(c % 2 == 0, c // 2, n_chip - 1 - c // 2)

    def chip_at(p):
        return jnp.where(p < n_chip // 2, 2 * p, 2 * (n_chip - 1 - p) + 1)

    here = place(chip)
    turn = 1 - 2 * core
    away = here - place(owner // 2)
    distance = (turn * away + n_chip) % n_chip
    distance_other = (n_chip - turn * away) % n_chip
    own_chip = owner // 2 == chip
    own_core = owner == index
    swap = swap_pairs(n_dev, 1)
    pairs = ring_pairs(n_chip)

    banks = [bank_s, bank_t]

    def tile_of(side, slot):
        return jnp.where(side == 0, slot, n_chunk - 1 - slot) * (STEP // 8)

    chunks = first_chunks(bank_s, bank_t, core)

    first = [None, None]
    for i in (1, 0):
        first[i] = jnp.where(own_core, chunks[i], lax.ppermute(chunks[2 + i], "wide", swap))

    def own_rows(i, j):
        if j < 2:
            return rows_at(first[i], jnp.where(core == 0, j, 1 - j) * (STEP // 8), STEP)
        return rows_at(full[i], tile_of(core, j), STEP)

    full = [None, None]
    pools = [jnp.zeros_like(bank_s), jnp.zeros_like(bank_t)]
    rows = put_rows(jnp.zeros((n_chip * block, width), passages.dtype), passages, 0)
    moving = [own_rows(i, 0) for i in range(2)]
    riding = [passages[:sub], passages[sub:]]

    def keep(i, t, sent):
        other = lax.ppermute(sent, "wide", swap)
        for side, away, piece in ((core, distance, sent), (1 - core, distance_other, other)):
            slot = t - away
            take = (slot >= 0) & (slot < n_chunk)
            at = tile_of(side, jnp.clip(slot, 0, n_chunk - 1))
            pools[i] = put_rows(pools[i], jnp.where(take, piece, rows_at(pools[i], at, STEP)), at)

    def arrive(i, t, got):
        nonlocal rows
        if t < n_chip - 1:
            riding[i] = got[STEP:]
            got = got[:STEP]
            origin = chip_at((here - turn * (t + 1) + n_chip) % n_chip)
            rows = put_rows(rows, riding[i], (origin ^ chip) * (block // 8) + i * (sub // 8))
        moving[i] = jnp.where(own_chip, own_rows(i, t + 1), got) if t + 1 < n_chunk else got

    lead, came = None, [None, None]
    for t in range(rounds):
        for i in (1, 0):
            if t:
                got, _ = lax.optimization_barrier((came[i], lead))
                arrive(i, t - 1, got)
            sent = jnp.concatenate([moving[i], riding[i]], 0) if t < n_chip - 1 else moving[i]
            if t == 0:
                bank, sent = lax.optimization_barrier((banks[i], sent))
                full[i] = jnp.where(own_core, bank, lax.ppermute(bank, "wide", swap))
                if i == 0:
                    sent, _ = lax.optimization_barrier((sent, lead))
            lead = sent
            came[i] = lax.ppermute(sent, "wide", pairs)
            keep(i, t, sent[:STEP])
    for i in (1, 0):
        arrive(i, rounds - 1, came[i])
    for i in (1, 0):
        keep(i, rounds, moving[i])
    return pools[0], pools[1], rows


def dot_t(a, b):
    return lax.dot_general(a, b, (((1,), (1,)), ((), ())), preferred_element_type=jnp.float32)


def tail_kernel(scale, n_rows, *refs):
    pass_refs, refs = refs[:n_rows], refs[n_rows:]
    q, tq, pool_s, pool_t, mask, column = refs[:6]
    gp, gq, loss, pieces = refs[6:]
    n_query, width = q.shape
    first = 0
    for ref in pass_refs:
        pieces[first : first + ref.shape[0], :] = ref[...]
        first += ref.shape[0]
    block = min(256, n_query)

    @pl.loop(0, n_query // block)
    def _(b):
        at = pl.ds(pl.multiple_of(b * block, block), block)
        p = dot_t(q[at, :], pieces[...]) * scale
        z = dot_t(q[at, :], pool_s[...]) * scale
        tt = dot_t(tq[at, :], pool_t[...]) * scale
        weight = mask[at, :].astype(jnp.float32) * jax.nn.sigmoid(-tt)
        top = jnp.maximum(jnp.max(p, axis=1, keepdims=True), jnp.max(z, axis=1, keepdims=True))
        total = jnp.sum(jnp.exp(p - top), axis=1, keepdims=True) + jnp.sum(
            weight * jnp.exp(z - top), axis=1, keepdims=True
        )
        lse = top + jnp.log(total)
        hit = (lax.broadcasted_iota(jnp.int32, p.shape, 1) == column[at, :]).astype(jnp.float32)
        loss[at, :] = lse - jnp.sum(p * hit, axis=1, keepdims=True)
        gp[at, :] = (jnp.exp(p - lse) - hit).astype(jnp.bfloat16)
        gq[at, :] = (weight * jnp.exp(z - lse)).astype(jnp.bfloat16)


def tail(scale, pass_parts, queries, teacher, pool_s, pool_t, mask, column):
    n_query, width = queries.shape
    n_pass = sum(p.shape[0] for p in pass_parts)
    pool = pool_s.shape[0]
    bf16, f32 = jnp.bfloat16, jnp.float32
    arrays = [*pass_parts, queries, teacher, pool_s, pool_t, mask, column]
    vmem = pl.BlockSpec(memory_space=pltpu.VMEM)
    return pl.pallas_call(
        functools.partial(tail_kernel, scale, len(pass_parts)),
        out_shape=[
            jax.ShapeDtypeStruct((n_query, n_pass), bf16),
            jax.ShapeDtypeStruct((n_query, pool), bf16),
            jax.ShapeDtypeStruct((n_query, 1), f32),
            jax.ShapeDtypeStruct((n_pass, width), bf16),
        ],
        in_specs=[vmem] * len(arrays),
        out_specs=[vmem] * 4,
        compiler_params=pltpu.CompilerParams(vmem_limit_bytes=VMEM_LIMIT),
        cost_estimate=pl.CostEstimate(
            flops=2 * n_query * width * (n_pass + 2 * pool),
            bytes_accessed=4 * width * (n_query + 2 * n_pass + pool),
            transcendentals=0,
        ),
        name="scores",
    )(*arrays)


def body(
    queries, teacher_queries, passages, bank_student, bank_teacher, owner, positives, keep_mask
):
    n_dev = lax.axis_size("wide")
    n_chip = n_dev // 2
    n_dp = lax.axis_size("dp")
    index = lax.axis_index("wide")
    replica = lax.axis_index("dp")
    core = index % 2
    chip = index // 2
    block, width = passages.shape
    scale = 2.0 / math.sqrt(width)
    n_pass = block * n_dev
    swap = swap_pairs(n_dev, 1)
    across = [(0, 1), (1, 0)]
    pool_s, pool_t, rows = gather_rows(bank_student, bank_teacher, passages, owner[0], index, core)
    pass_parts = [rows, lax.ppermute(rows, "wide", swap)]
    chip_of = (positives // (2 * block)) ^ chip
    core_of = ((positives // block) % 2) ^ core
    column = (core_of * n_chip + chip_of) * block + positives % block
    grad_p, grad_q, row_loss, pieces = tail(
        scale, pass_parts, queries, teacher_queries, pool_s, pool_t, keep_mask, column[:, None]
    )

    chip_bits = ["x"] + ["z%d" % b for b in range(n_chip.bit_length() - 2)]
    pairs_of = {name: swap_pairs(n_dev, 2 << b) for b, name in enumerate(chip_bits)}
    zs = chip_bits[1:]
    orders = (["x"] + zs, zs[:1] + ["x"] + zs[1:])
    lefts = [chip_bits[::-1], chip_bits[::-1]]
    sums = []
    sent = [None, None]
    mid, half = n_pass // 2, width // 2
    for h in range(2):
        columns = queries[:, h * half : (h + 1) * half]

        def terms(grads):
            return lax.dot_general(
                grads, columns, (((0,), (0,)), ((), ())), preferred_element_type=jnp.float32
            )

        got = lax.ppermute(terms(grad_p[:, mid:]).astype(jnp.bfloat16), "wide", swap)
        sums.append((terms(grad_p[:, :mid]) + got.astype(jnp.float32)).reshape((2,) * len(chip_bits) + (block, half)))
    pending = None
    for step in range(len(chip_bits)):
        for h in range(2):
            if h == 1 and step:
                pending, _ = lax.optimization_barrier((pending, sent[0]))
                sums[1] = sums[1] + pending.astype(jnp.float32)
            at = lefts[h].index(orders[h][step])
            sent[h] = lax.index_in_dim(sums[h], 1, at, keepdims=False).astype(jnp.bfloat16)
            sums[h] = lax.index_in_dim(sums[h], 0, at, keepdims=False)
            lefts[h].pop(at)
            if h == 1 and step == 0:
                sent[1], _ = lax.optimization_barrier((sent[1], sent[0]))
            got = lax.ppermute(sent[h], "wide", pairs_of[orders[h][step]])
            if h == 0:
                sums[0] = sums[0] + got.astype(jnp.float32)
            else:
                pending = got
        if step == 0:
            (late_p, grad_q, row_loss), _ = lax.optimization_barrier(((grad_p, grad_q, row_loss), sent[1]))
    pending, _ = lax.optimization_barrier((pending, sums[0]))
    sums[1] = sums[1] + pending.astype(jnp.float32)
    if n_dp == 2:
        sums = [x + lax.ppermute(x, "dp", across) for x in sums]
    else:
        sums = [lax.psum(x, "dp") for x in sums]
    passage_grad = jnp.concatenate(sums, 1) * scale

    qgrad = jnp.dot(late_p, pieces, preferred_element_type=jnp.float32) + jnp.dot(
        grad_q, pool_s, preferred_element_type=jnp.float32
    )
    query_grad = (qgrad * scale).astype(jnp.bfloat16)
    return (row_loss[:, 0], query_grad, passage_grad)


def solution(mesh):
    placed = (
        P(("wide", "dp"), None),
        P(("wide", "dp"), None),
        P("wide", None),
        P("wide", None),
        P("wide", None),
        P("dp"),
        P(("wide", "dp")),
        P(("wide", "dp"), None),
    )
    return jax.shard_map(
        body,
        mesh=mesh,
        in_specs=placed,
        out_specs=(P(("wide", "dp")), P(("wide", "dp"), None), P("wide", None)),
        check_vma=False,
    )
```

```python
import functools
import math

import jax
import jax.numpy as jnp
from jax import lax
from jax.experimental import pallas as pl
from jax.experimental.pallas import tpu as pltpu
from jax.sharding import PartitionSpec as P

STEP = 32
VMEM_LIMIT = 24 * 2**20


def ring_order(n_chip):
    nz = n_chip // 2
    return [2 * z for z in range(nz)] + [2 * z + 1 for z in reversed(range(nz))]


def ring_pairs(n_chip):
    order = ring_order(n_chip)
    pairs = []
    for i, chip in enumerate(order):
        pairs.append((2 * chip, 2 * order[(i + 1) % n_chip]))
        pairs.append((2 * chip + 1, 2 * order[(i - 1) % n_chip] + 1))
    return pairs


def swap_pairs(n, bit):
    return [(i, i ^ bit) for i in range(n)]


def rows_at(x, tile, count):
    return lax.dynamic_slice_in_dim(x, tile * 8, count, 0)


def put_rows(x, rows, tile):
    return lax.dynamic_update_slice_in_dim(x, rows, tile * 8, 0)


def first_kernel(side_ref, bank_s, bank_t, *refs):
    outs = refs
    pool = bank_s.shape[0]
    for n, out in enumerate(outs):
        side = side_ref[0] if n < 2 else 1 - side_ref[0]
        at = pl.multiple_of(side * (pool - 2 * STEP), STEP)
        out[...] = (bank_s, bank_t)[n % 2][pl.ds(at, 2 * STEP), :]


def first_chunks(bank_s, bank_t, core):
    chunk = jax.ShapeDtypeStruct((2 * STEP, bank_s.shape[1]), bank_s.dtype)
    return pl.pallas_call(
        first_kernel,
        out_shape=[chunk] * 4,
        in_specs=[pl.BlockSpec(memory_space=pltpu.SMEM)] + [pl.BlockSpec(memory_space=pltpu.VMEM)] * 2,
        out_specs=[pl.BlockSpec(memory_space=pltpu.VMEM)] * 4,
        compiler_params=pltpu.CompilerParams(vmem_limit_bytes=VMEM_LIMIT),
        name="first_chunks",
    )(core.astype(jnp.int32)[None], bank_s, bank_t)


def gather_rows(bank_s, bank_t, passages, owner, index, core):
    n_dev = lax.axis_size("wide")
    n_chip = n_dev // 2
    pool, width = bank_s.shape
    n_chunk = pool // STEP
    rounds = max((n_chunk + n_chip - 1) // 2, n_chip - 1)
    block = passages.shape[0]
    sub = block // 2
    chip = index // 2

    def place(c):
        return jnp.where(c % 2 == 0, c // 2, n_chip - 1 - c // 2)

    def chip_at(p):
        return jnp.where(p < n_chip // 2, 2 * p, 2 * (n_chip - 1 - p) + 1)

    here = place(chip)
    turn = 1 - 2 * core
    away = here - place(owner // 2)
    distance = (turn * away + n_chip) % n_chip
    distance_other = (n_chip - turn * away) % n_chip
    own_chip = owner // 2 == chip
    own_core = owner == index
    swap = swap_pairs(n_dev, 1)
    pairs = ring_pairs(n_chip)

    banks = [bank_s, bank_t]

    def tile_of(side, slot):
        return jnp.where(side == 0, slot, n_chunk - 1 - slot) * (STEP // 8)

    chunks = first_chunks(bank_s, bank_t, core)

    first = [None, None]
    for i in (1, 0):
        first[i] = jnp.where(own_core, chunks[i], lax.ppermute(chunks[2 + i], "wide", swap))

    full = [None, None]
    for i in (1, 0):
        bank, first[0] = lax.optimization_barrier((banks[i], first[0]))
        full[i] = jnp.where(own_core, bank, lax.ppermute(bank, "wide", swap))

    def own_rows(i, j):
        if j < 2:
            return rows_at(first[i], jnp.where(core == 0, j, 1 - j) * (STEP // 8), STEP)
        return rows_at(full[i], tile_of(core, j), STEP)

    pools = [jnp.zeros_like(bank_s), jnp.zeros_like(bank_t)]
    rows = put_rows(jnp.zeros((n_chip * block, width), passages.dtype), passages, 0)
    moving = [own_rows(i, 0) for i in range(2)]
    riding = [passages[:sub], passages[sub:]]

    def keep(i, t, sent):
        other = lax.ppermute(sent, "wide", swap)
        for side, away, piece in ((core, distance, sent), (1 - core, distance_other, other)):
            slot = t - away
            take = (slot >= 0) & (slot < n_chunk)
            at = tile_of(side, jnp.clip(slot, 0, n_chunk - 1))
            pools[i] = put_rows(pools[i], jnp.where(take, piece, rows_at(pools[i], at, STEP)), at)

    def arrive(i, t, got):
        nonlocal rows
        if t < n_chip - 1:
            riding[i] = got[STEP:]
            got = got[:STEP]
            origin = chip_at((here - turn * (t + 1) + n_chip) % n_chip)
            rows = put_rows(rows, riding[i], (origin ^ chip) * (block // 8) + i * (sub // 8))
        moving[i] = jnp.where(own_chip, own_rows(i, t + 1), got) if t + 1 < n_chunk else got

    lead, came = None, [None, None]
    for t in range(rounds):
        for i in (1, 0):
            if t:
                got, _ = lax.optimization_barrier((came[i], lead))
                arrive(i, t - 1, got)
            sent = jnp.concatenate([moving[i], riding[i]], 0) if t < n_chip - 1 else moving[i]
            if t == 0 and i == 0:
                sent, _ = lax.optimization_barrier((sent, lead))
            lead = sent
            came[i] = lax.ppermute(sent, "wide", pairs)
            keep(i, t, sent[:STEP])
    for i in (1, 0):
        arrive(i, rounds - 1, came[i])
    for i in (1, 0):
        keep(i, rounds, moving[i])
    return pools[0], pools[1], rows


def dot_t(a, b):
    return lax.dot_general(a, b, (((1,), (1,)), ((), ())), preferred_element_type=jnp.float32)


def tail_kernel(scale, n_rows, *refs):
    pass_refs, refs = refs[:n_rows], refs[n_rows:]
    q, tq, pool_s, pool_t, mask, column = refs[:6]
    gp, gq, loss, pieces = refs[6:]
    n_query, width = q.shape
    first = 0
    for ref in pass_refs:
        pieces[first : first + ref.shape[0], :] = ref[...]
        first += ref.shape[0]
    block = min(256, n_query)

    @pl.loop(0, n_query // block)
    def _(b):
        at = pl.ds(pl.multiple_of(b * block, block), block)
        p = dot_t(q[at, :], pieces[...]) * scale
        z = dot_t(q[at, :], pool_s[...]) * scale
        tt = dot_t(tq[at, :], pool_t[...]) * scale
        weight = mask[at, :].astype(jnp.float32) * jax.nn.sigmoid(-tt)
        top = jnp.maximum(jnp.max(p, axis=1, keepdims=True), jnp.max(z, axis=1, keepdims=True))
        total = jnp.sum(jnp.exp(p - top), axis=1, keepdims=True) + jnp.sum(
            weight * jnp.exp(z - top), axis=1, keepdims=True
        )
        lse = top + jnp.log(total)
        hit = (lax.broadcasted_iota(jnp.int32, p.shape, 1) == column[at, :]).astype(jnp.float32)
        loss[at, :] = lse - jnp.sum(p * hit, axis=1, keepdims=True)
        gp[at, :] = (jnp.exp(p - lse) - hit).astype(jnp.bfloat16)
        gq[at, :] = (weight * jnp.exp(z - lse)).astype(jnp.bfloat16)


def tail(scale, pass_parts, queries, teacher, pool_s, pool_t, mask, column):
    n_query, width = queries.shape
    n_pass = sum(p.shape[0] for p in pass_parts)
    pool = pool_s.shape[0]
    bf16, f32 = jnp.bfloat16, jnp.float32
    arrays = [*pass_parts, queries, teacher, pool_s, pool_t, mask, column]
    vmem = pl.BlockSpec(memory_space=pltpu.VMEM)
    return pl.pallas_call(
        functools.partial(tail_kernel, scale, len(pass_parts)),
        out_shape=[
            jax.ShapeDtypeStruct((n_query, n_pass), bf16),
            jax.ShapeDtypeStruct((n_query, pool), bf16),
            jax.ShapeDtypeStruct((n_query, 1), f32),
            jax.ShapeDtypeStruct((n_pass, width), bf16),
        ],
        in_specs=[vmem] * len(arrays),
        out_specs=[vmem] * 4,
        compiler_params=pltpu.CompilerParams(vmem_limit_bytes=VMEM_LIMIT),
        cost_estimate=pl.CostEstimate(
            flops=2 * n_query * width * (n_pass + 2 * pool),
            bytes_accessed=4 * width * (n_query + 2 * n_pass + pool),
            transcendentals=0,
        ),
        name="scores",
    )(*arrays)


def body(
    queries, teacher_queries, passages, bank_student, bank_teacher, owner, positives, keep_mask
):
    n_dev = lax.axis_size("wide")
    n_chip = n_dev // 2
    n_dp = lax.axis_size("dp")
    index = lax.axis_index("wide")
    replica = lax.axis_index("dp")
    core = index % 2
    chip = index // 2
    block, width = passages.shape
    scale = 2.0 / math.sqrt(width)
    n_pass = block * n_dev
    swap = swap_pairs(n_dev, 1)
    across = [(0, 1), (1, 0)]
    pool_s, pool_t, rows = gather_rows(bank_student, bank_teacher, passages, owner[0], index, core)
    pass_parts = [rows, lax.ppermute(rows, "wide", swap)]
    chip_of = (positives // (2 * block)) ^ chip
    core_of = ((positives // block) % 2) ^ core
    column = (core_of * n_chip + chip_of) * block + positives % block
    grad_p, grad_q, row_loss, pieces = tail(
        scale, pass_parts, queries, teacher_queries, pool_s, pool_t, keep_mask, column[:, None]
    )

    chip_bits = ["x"] + ["z%d" % b for b in range(n_chip.bit_length() - 2)]
    pairs_of = {name: swap_pairs(n_dev, 2 << b) for b, name in enumerate(chip_bits)}
    zs = chip_bits[1:]
    orders = (["x"] + zs, zs[:1] + ["x"] + zs[1:])
    lefts = [chip_bits[::-1], chip_bits[::-1]]
    sums = []
    sent = [None, None]
    mid, half = n_pass // 2, width // 2
    for h in range(2):
        columns = queries[:, h * half : (h + 1) * half]

        def terms(grads):
            return lax.dot_general(
                grads, columns, (((0,), (0,)), ((), ())), preferred_element_type=jnp.float32
            )

        got = lax.ppermute(terms(grad_p[:, mid:]).astype(jnp.bfloat16), "wide", swap)
        sums.append((terms(grad_p[:, :mid]) + got.astype(jnp.float32)).reshape((2,) * len(chip_bits) + (block, half)))
    pending = None
    for step in range(len(chip_bits)):
        for h in range(2):
            if h == 1 and step:
                pending, _ = lax.optimization_barrier((pending, sent[0]))
                sums[1] = sums[1] + pending.astype(jnp.float32)
            at = lefts[h].index(orders[h][step])
            sent[h] = lax.index_in_dim(sums[h], 1, at, keepdims=False).astype(jnp.bfloat16)
            sums[h] = lax.index_in_dim(sums[h], 0, at, keepdims=False)
            lefts[h].pop(at)
            if h == 1 and step == 0:
                sent[1], _ = lax.optimization_barrier((sent[1], sent[0]))
            got = lax.ppermute(sent[h], "wide", pairs_of[orders[h][step]])
            if h == 0:
                sums[0] = sums[0] + got.astype(jnp.float32)
            else:
                pending = got
        if step == 0:
            (late_p, grad_q, row_loss), _ = lax.optimization_barrier(((grad_p, grad_q, row_loss), sent[1]))
    pending, _ = lax.optimization_barrier((pending, sums[0]))
    sums[1] = sums[1] + pending.astype(jnp.float32)
    if n_dp == 2:
        sums = [x + lax.ppermute(x, "dp", across) for x in sums]
    else:
        sums = [lax.psum(x, "dp") for x in sums]
    passage_grad = jnp.concatenate(sums, 1) * scale

    qgrad = jnp.dot(late_p, pieces, preferred_element_type=jnp.float32) + jnp.dot(
        grad_q, pool_s, preferred_element_type=jnp.float32
    )
    query_grad = (qgrad * scale).astype(jnp.bfloat16)
    return (row_loss[:, 0], query_grad, passage_grad)


def solution(mesh):
    placed = (
        P(("wide", "dp"), None),
        P(("wide", "dp"), None),
        P("wide", None),
        P("wide", None),
        P("wide", None),
        P("dp"),
        P(("wide", "dp")),
        P(("wide", "dp"), None),
    )
    return jax.shard_map(
        body,
        mesh=mesh,
        in_specs=placed,
        out_specs=(P(("wide", "dp")), P(("wide", "dp"), None), P("wide", None)),
        check_vma=False,
    )
```

```python
import functools
import math

import jax
import jax.numpy as jnp
from jax import lax
from jax.experimental import pallas as pl
from jax.experimental.pallas import tpu as pltpu
from jax.sharding import PartitionSpec as P

STEP = 32
VMEM_LIMIT = 24 * 2**20


def ring_order(n_chip):
    nz = n_chip // 2
    return [2 * z for z in range(nz)] + [2 * z + 1 for z in reversed(range(nz))]


def ring_pairs(n_chip):
    order = ring_order(n_chip)
    pairs = []
    for i, chip in enumerate(order):
        pairs.append((2 * chip, 2 * order[(i + 1) % n_chip]))
        pairs.append((2 * chip + 1, 2 * order[(i - 1) % n_chip] + 1))
    return pairs


def swap_pairs(n, bit):
    return [(i, i ^ bit) for i in range(n)]


def rows_at(x, tile, count):
    return lax.dynamic_slice_in_dim(x, tile * 8, count, 0)


def put_rows(x, rows, tile):
    return lax.dynamic_update_slice_in_dim(x, rows, tile * 8, 0)


def first_kernel(side_ref, bank_s, bank_t, *refs):
    outs = refs
    pool = bank_s.shape[0]
    for n, out in enumerate(outs):
        side = side_ref[0] if n < 2 else 1 - side_ref[0]
        at = pl.multiple_of(side * (pool - 2 * STEP), STEP)
        out[...] = (bank_s, bank_t)[n % 2][pl.ds(at, 2 * STEP), :]


def first_chunks(bank_s, bank_t, core):
    chunk = jax.ShapeDtypeStruct((2 * STEP, bank_s.shape[1]), bank_s.dtype)
    return pl.pallas_call(
        first_kernel,
        out_shape=[chunk] * 4,
        in_specs=[pl.BlockSpec(memory_space=pltpu.SMEM)] + [pl.BlockSpec(memory_space=pltpu.VMEM)] * 2,
        out_specs=[pl.BlockSpec(memory_space=pltpu.VMEM)] * 4,
        compiler_params=pltpu.CompilerParams(vmem_limit_bytes=VMEM_LIMIT),
        name="first_chunks",
    )(core.astype(jnp.int32)[None], bank_s, bank_t)


def gather_rows(bank_s, bank_t, passages, owner, index, core):
    n_dev = lax.axis_size("wide")
    n_chip = n_dev // 2
    pool, width = bank_s.shape
    n_chunk = pool // STEP
    rounds = max((n_chunk + n_chip - 1) // 2, n_chip - 1)
    block = passages.shape[0]
    sub = block // 2
    chip = index // 2

    def place(c):
        return jnp.where(c % 2 == 0, c // 2, n_chip - 1 - c // 2)

    def chip_at(p):
        return jnp.where(p < n_chip // 2, 2 * p, 2 * (n_chip - 1 - p) + 1)

    here = place(chip)
    turn = 1 - 2 * core
    away = here - place(owner // 2)
    distance = (turn * away + n_chip) % n_chip
    distance_other = (n_chip - turn * away) % n_chip
    own_chip = owner // 2 == chip
    own_core = owner == index
    swap = swap_pairs(n_dev, 1)
    pairs = ring_pairs(n_chip)

    banks = [bank_s, bank_t]

    def tile_of(side, slot):
        return jnp.where(side == 0, slot, n_chunk - 1 - slot) * (STEP // 8)

    chunks = first_chunks(bank_s, bank_t, core)

    first = [None, None]
    for i in (1, 0):
        first[i] = jnp.where(own_core, chunks[i], lax.ppermute(chunks[2 + i], "wide", swap))

    full = [None, None]
    for i in (1, 0):
        bank, first[0] = lax.optimization_barrier((banks[i], first[0]))
        full[i] = jnp.where(own_core, bank, lax.ppermute(bank, "wide", swap))

    def own_rows(i, j):
        if j < 2:
            return rows_at(first[i], jnp.where(core == 0, j, 1 - j) * (STEP // 8), STEP)
        return rows_at(full[i], tile_of(core, j), STEP)

    pools = [jnp.zeros_like(bank_s), jnp.zeros_like(bank_t)]
    rows = put_rows(jnp.zeros((n_chip * block, width), passages.dtype), passages, 0)
    moving = [own_rows(i, 0) for i in range(2)]
    riding = [passages[:sub], passages[sub:]]

    def keep(i, t, sent, other=None):
        if other is None:
            other = lax.ppermute(sent, "wide", swap)
        for side, away, piece in ((core, distance, sent), (1 - core, distance_other, other)):
            slot = t - away
            take = (slot >= 0) & (slot < n_chunk)
            at = tile_of(side, jnp.clip(slot, 0, n_chunk - 1))
            pools[i] = put_rows(pools[i], jnp.where(take, piece, rows_at(pools[i], at, STEP)), at)

    def arrive(i, t, got):
        nonlocal rows
        if t < n_chip - 1:
            riding[i] = got[STEP:]
            got = got[:STEP]
            origin = chip_at((here - turn * (t + 1) + n_chip) % n_chip)
            rows = put_rows(rows, riding[i], (origin ^ chip) * (block // 8) + i * (sub // 8))
        moving[i] = jnp.where(own_chip, own_rows(i, t + 1), got) if t + 1 < n_chunk else got

    lead, came = None, [None, None]
    for t in range(rounds):
        for i in (1, 0):
            if t:
                got, _ = lax.optimization_barrier((came[i], lead))
                arrive(i, t - 1, got)
            sent = jnp.concatenate([moving[i], riding[i]], 0) if t < n_chip - 1 else moving[i]
            if t == 0 and i == 0:
                sent, _ = lax.optimization_barrier((sent, lead))
            lead = sent
            came[i] = lax.ppermute(sent, "wide", pairs)
            keep(i, t, sent[:STEP])
    rows_other = lax.ppermute(rows, "wide", swap)
    for i in (1, 0):
        arrive(i, rounds - 1, came[i])
    for i in (1, 0):
        if rounds > n_chip - 1:
            keep(i, rounds, moving[i])
            continue
        other = lax.ppermute(jnp.concatenate([riding[i], moving[i]], 0), "wide", swap)
        origin = chip_at((here + turn * rounds + n_chip) % n_chip)
        rows_other = put_rows(rows_other, other[:sub], (origin ^ chip) * (block // 8) + i * (sub // 8))
        keep(i, rounds, moving[i], other[sub:])
    return pools[0], pools[1], [rows, rows_other]


def dot_t(a, b):
    return lax.dot_general(a, b, (((1,), (1,)), ((), ())), preferred_element_type=jnp.float32)


def tail_kernel(scale, n_rows, *refs):
    pass_refs, refs = refs[:n_rows], refs[n_rows:]
    q, tq, pool_s, pool_t, mask, column = refs[:6]
    gp, gq, loss, pieces = refs[6:]
    n_query, width = q.shape
    first = 0
    for ref in pass_refs:
        pieces[first : first + ref.shape[0], :] = ref[...]
        first += ref.shape[0]
    block = min(256, n_query)

    @pl.loop(0, n_query // block)
    def _(b):
        at = pl.ds(pl.multiple_of(b * block, block), block)
        p = dot_t(q[at, :], pieces[...]) * scale
        z = dot_t(q[at, :], pool_s[...]) * scale
        tt = dot_t(tq[at, :], pool_t[...]) * scale
        weight = mask[at, :].astype(jnp.float32) * jax.nn.sigmoid(-tt)
        top = jnp.maximum(jnp.max(p, axis=1, keepdims=True), jnp.max(z, axis=1, keepdims=True))
        total = jnp.sum(jnp.exp(p - top), axis=1, keepdims=True) + jnp.sum(
            weight * jnp.exp(z - top), axis=1, keepdims=True
        )
        lse = top + jnp.log(total)
        hit = (lax.broadcasted_iota(jnp.int32, p.shape, 1) == column[at, :]).astype(jnp.float32)
        loss[at, :] = lse - jnp.sum(p * hit, axis=1, keepdims=True)
        gp[at, :] = (jnp.exp(p - lse) - hit).astype(jnp.bfloat16)
        gq[at, :] = (weight * jnp.exp(z - lse)).astype(jnp.bfloat16)


def tail(scale, pass_parts, queries, teacher, pool_s, pool_t, mask, column):
    n_query, width = queries.shape
    n_pass = sum(p.shape[0] for p in pass_parts)
    pool = pool_s.shape[0]
    bf16, f32 = jnp.bfloat16, jnp.float32
    arrays = [*pass_parts, queries, teacher, pool_s, pool_t, mask, column]
    vmem = pl.BlockSpec(memory_space=pltpu.VMEM)
    return pl.pallas_call(
        functools.partial(tail_kernel, scale, len(pass_parts)),
        out_shape=[
            jax.ShapeDtypeStruct((n_query, n_pass), bf16),
            jax.ShapeDtypeStruct((n_query, pool), bf16),
            jax.ShapeDtypeStruct((n_query, 1), f32),
            jax.ShapeDtypeStruct((n_pass, width), bf16),
        ],
        in_specs=[vmem] * len(arrays),
        out_specs=[vmem] * 4,
        compiler_params=pltpu.CompilerParams(vmem_limit_bytes=VMEM_LIMIT),
        cost_estimate=pl.CostEstimate(
            flops=2 * n_query * width * (n_pass + 2 * pool),
            bytes_accessed=4 * width * (n_query + 2 * n_pass + pool),
            transcendentals=0,
        ),
        name="scores",
    )(*arrays)


def body(
    queries, teacher_queries, passages, bank_student, bank_teacher, owner, positives, keep_mask
):
    n_dev = lax.axis_size("wide")
    n_chip = n_dev // 2
    n_dp = lax.axis_size("dp")
    index = lax.axis_index("wide")
    replica = lax.axis_index("dp")
    core = index % 2
    chip = index // 2
    block, width = passages.shape
    scale = 2.0 / math.sqrt(width)
    n_pass = block * n_dev
    swap = swap_pairs(n_dev, 1)
    across = [(0, 1), (1, 0)]
    pool_s, pool_t, pass_parts = gather_rows(bank_student, bank_teacher, passages, owner[0], index, core)
    chip_of = (positives // (2 * block)) ^ chip
    core_of = ((positives // block) % 2) ^ core
    column = (core_of * n_chip + chip_of) * block + positives % block
    grad_p, grad_q, row_loss, pieces = tail(
        scale, pass_parts, queries, teacher_queries, pool_s, pool_t, keep_mask, column[:, None]
    )

    chip_bits = ["x"] + ["z%d" % b for b in range(n_chip.bit_length() - 2)]
    pairs_of = {name: swap_pairs(n_dev, 2 << b) for b, name in enumerate(chip_bits)}
    zs = chip_bits[1:]
    orders = (["x"] + zs, zs[:1] + ["x"] + zs[1:])
    lefts = [chip_bits[::-1], chip_bits[::-1]]
    sums = []
    sent = [None, None]
    mid, half = n_pass // 2, width // 2
    for h in range(2):
        columns = queries[:, h * half : (h + 1) * half]

        def terms(grads):
            return lax.dot_general(
                grads, columns, (((0,), (0,)), ((), ())), preferred_element_type=jnp.float32
            )

        got = lax.ppermute(terms(grad_p[:, mid:]).astype(jnp.bfloat16), "wide", swap)
        sums.append((terms(grad_p[:, :mid]) + got.astype(jnp.float32)).reshape((2,) * len(chip_bits) + (block, half)))
    pending = None
    for step in range(len(chip_bits)):
        for h in range(2):
            if h == 1 and step:
                pending, _ = lax.optimization_barrier((pending, sent[0]))
                sums[1] = sums[1] + pending.astype(jnp.float32)
            at = lefts[h].index(orders[h][step])
            sent[h] = lax.index_in_dim(sums[h], 1, at, keepdims=False).astype(jnp.bfloat16)
            sums[h] = lax.index_in_dim(sums[h], 0, at, keepdims=False)
            lefts[h].pop(at)
            if h == 1 and step == 0:
                sent[1], _ = lax.optimization_barrier((sent[1], sent[0]))
            got = lax.ppermute(sent[h], "wide", pairs_of[orders[h][step]])
            if h == 0:
                sums[0] = sums[0] + got.astype(jnp.float32)
            else:
                pending = got
        if step == 0:
            (late_p, grad_q, row_loss), _ = lax.optimization_barrier(((grad_p, grad_q, row_loss), sent[1]))
    pending, _ = lax.optimization_barrier((pending, sums[0]))
    sums[1] = sums[1] + pending.astype(jnp.float32)
    if n_dp == 2:
        sums = [x + lax.ppermute(x, "dp", across) for x in sums]
    else:
        sums = [lax.psum(x, "dp") for x in sums]
    passage_grad = jnp.concatenate(sums, 1) * scale

    qgrad = jnp.dot(late_p, pieces, preferred_element_type=jnp.float32) + jnp.dot(
        grad_q, pool_s, preferred_element_type=jnp.float32
    )
    query_grad = (qgrad * scale).astype(jnp.bfloat16)
    return (row_loss[:, 0], query_grad, passage_grad)


def solution(mesh):
    placed = (
        P(("wide", "dp"), None),
        P(("wide", "dp"), None),
        P("wide", None),
        P("wide", None),
        P("wide", None),
        P("dp"),
        P(("wide", "dp")),
        P(("wide", "dp"), None),
    )
    return jax.shard_map(
        body,
        mesh=mesh,
        in_specs=placed,
        out_specs=(P(("wide", "dp")), P(("wide", "dp"), None), P("wide", None)),
        check_vma=False,
    )
```

```python
import functools
import math

import jax
import jax.numpy as jnp
from jax import lax
from jax.experimental import pallas as pl
from jax.experimental.pallas import tpu as pltpu
from jax.sharding import PartitionSpec as P

STEP = 32
VMEM_LIMIT = 24 * 2**20


def ring_order(n_chip):
    nz = n_chip // 2
    return [2 * z for z in range(nz)] + [2 * z + 1 for z in reversed(range(nz))]


def ring_pairs(n_chip):
    order = ring_order(n_chip)
    pairs = []
    for i, chip in enumerate(order):
        pairs.append((2 * chip, 2 * order[(i + 1) % n_chip]))
        pairs.append((2 * chip + 1, 2 * order[(i - 1) % n_chip] + 1))
    return pairs


def swap_pairs(n, bit):
    return [(i, i ^ bit) for i in range(n)]


def rows_at(x, tile, count):
    return lax.dynamic_slice_in_dim(x, tile * 8, count, 0)


def put_rows(x, rows, tile):
    return lax.dynamic_update_slice_in_dim(x, rows, tile * 8, 0)


def first_kernel(side_ref, bank_s, bank_t, *refs):
    outs = refs
    pool = bank_s.shape[0]
    for n, out in enumerate(outs):
        side = side_ref[0] if n < 2 else 1 - side_ref[0]
        at = pl.multiple_of(side * (pool - 2 * STEP), STEP)
        out[...] = (bank_s, bank_t)[n % 2][pl.ds(at, 2 * STEP), :]


def first_chunks(bank_s, bank_t, core):
    chunk = jax.ShapeDtypeStruct((2 * STEP, bank_s.shape[1]), bank_s.dtype)
    return pl.pallas_call(
        first_kernel,
        out_shape=[chunk] * 4,
        in_specs=[pl.BlockSpec(memory_space=pltpu.SMEM)] + [pl.BlockSpec(memory_space=pltpu.VMEM)] * 2,
        out_specs=[pl.BlockSpec(memory_space=pltpu.VMEM)] * 4,
        compiler_params=pltpu.CompilerParams(vmem_limit_bytes=VMEM_LIMIT),
        name="first_chunks",
    )(core.astype(jnp.int32)[None], bank_s, bank_t)


def gather_rows(bank_s, bank_t, passages, owner, index, core):
    n_dev = lax.axis_size("wide")
    n_chip = n_dev // 2
    pool, width = bank_s.shape
    n_chunk = pool // STEP
    rounds = max((n_chunk + n_chip - 1) // 2, n_chip - 1)
    block = passages.shape[0]
    sub = block // 2
    chip = index // 2

    def place(c):
        return jnp.where(c % 2 == 0, c // 2, n_chip - 1 - c // 2)

    def chip_at(p):
        return jnp.where(p < n_chip // 2, 2 * p, 2 * (n_chip - 1 - p) + 1)

    here = place(chip)
    turn = 1 - 2 * core
    away = here - place(owner // 2)
    distance = (turn * away + n_chip) % n_chip
    distance_other = (n_chip - turn * away) % n_chip
    own_chip = owner // 2 == chip
    own_core = owner == index
    swap = swap_pairs(n_dev, 1)
    pairs = ring_pairs(n_chip)

    banks = [bank_s, bank_t]

    def tile_of(side, slot):
        return jnp.where(side == 0, slot, n_chunk - 1 - slot) * (STEP // 8)

    chunks = first_chunks(bank_s, bank_t, core)

    first = [None, None]
    for i in (1, 0):
        first[i] = jnp.where(own_core, chunks[i], lax.ppermute(chunks[2 + i], "wide", swap))

    full = [None, None]
    for i in (1, 0):
        bank, first[0] = lax.optimization_barrier((banks[i], first[0]))
        full[i] = jnp.where(own_core, bank, lax.ppermute(bank, "wide", swap))

    def own_rows(i, j):
        if j < 2:
            return rows_at(first[i], jnp.where(core == 0, j, 1 - j) * (STEP // 8), STEP)
        return rows_at(full[i], tile_of(core, j), STEP)

    pools = [jnp.zeros_like(bank_s), jnp.zeros_like(bank_t)]
    rows = put_rows(jnp.zeros((n_chip * block, width), passages.dtype), passages, 0)
    moving = [own_rows(i, 0) for i in range(2)]
    riding = [passages[:sub], passages[sub:]]

    def keep(i, t, sent, other=None):
        if other is None:
            other = lax.ppermute(sent, "wide", swap)
        for side, away, piece in ((core, distance, sent), (1 - core, distance_other, other)):
            slot = t - away
            take = (slot >= 0) & (slot < n_chunk)
            at = tile_of(side, jnp.clip(slot, 0, n_chunk - 1))
            pools[i] = put_rows(pools[i], jnp.where(take, piece, rows_at(pools[i], at, STEP)), at)

    def arrive(i, t, got):
        nonlocal rows
        if t < n_chip - 1:
            riding[i] = got[STEP:]
            got = got[:STEP]
            origin = chip_at((here - turn * (t + 1) + n_chip) % n_chip)
            rows = put_rows(rows, riding[i], (origin ^ chip) * (block // 8) + i * (sub // 8))
        moving[i] = jnp.where(own_chip, own_rows(i, t + 1), got) if t + 1 < n_chunk else got

    lead, came = None, [None, None]
    for t in range(rounds):
        for i in (1, 0):
            if t:
                got, _ = lax.optimization_barrier((came[i], lead))
                arrive(i, t - 1, got)
            sent = jnp.concatenate([moving[i], riding[i]], 0) if t < n_chip - 1 else moving[i]
            if t == 0 and i == 0:
                sent, _ = lax.optimization_barrier((sent, lead))
            lead = sent
            came[i] = lax.ppermute(sent, "wide", pairs)
            keep(i, t, sent[:STEP])
    rows_other = lax.ppermute(rows, "wide", swap)
    for i in (1, 0):
        arrive(i, rounds - 1, came[i])
    for i in (1, 0):
        if rounds > n_chip - 1:
            keep(i, rounds, moving[i])
            continue
        other = lax.ppermute(jnp.concatenate([riding[i], moving[i]], 0), "wide", swap)
        origin = chip_at((here + turn * rounds + n_chip) % n_chip)
        rows_other = put_rows(rows_other, other[:sub], (origin ^ chip) * (block // 8) + i * (sub // 8))
        keep(i, rounds, moving[i], other[sub:])
    return pools[0], pools[1], [rows, rows_other]


def dot_t(a, b):
    return lax.dot_general(a, b, (((1,), (1,)), ((), ())), preferred_element_type=jnp.float32)


def tail_kernel(scale, n_rows, *refs):
    pass_refs, refs = refs[:n_rows], refs[n_rows:]
    q, tq, pool_s, pool_t, mask, column = refs[:6]
    gp, gq, loss, pieces = refs[6:]
    n_query, width = q.shape
    first = 0
    for ref in pass_refs:
        pieces[first : first + ref.shape[0], :] = ref[...]
        first += ref.shape[0]
    block = min(256, n_query)

    @pl.loop(0, n_query // block)
    def _(b):
        at = pl.ds(pl.multiple_of(b * block, block), block)
        p = dot_t(q[at, :], pieces[...]) * scale
        z = dot_t(q[at, :], pool_s[...]) * scale
        tt = dot_t(tq[at, :], pool_t[...]) * scale
        weight = mask[at, :].astype(jnp.float32) * jax.nn.sigmoid(-tt)
        top = jnp.maximum(jnp.max(p, axis=1, keepdims=True), jnp.max(z, axis=1, keepdims=True))
        total = jnp.sum(jnp.exp(p - top), axis=1, keepdims=True) + jnp.sum(
            weight * jnp.exp(z - top), axis=1, keepdims=True
        )
        lse = top + jnp.log(total)
        hit = (lax.broadcasted_iota(jnp.int32, p.shape, 1) == column[at, :]).astype(jnp.float32)
        loss[at, :] = lse - jnp.sum(p * hit, axis=1, keepdims=True)
        gp[at, :] = (jnp.exp(p - lse) - hit).astype(jnp.bfloat16)
        gq[at, :] = (weight * jnp.exp(z - lse)).astype(jnp.bfloat16)


def tail(scale, pass_parts, queries, teacher, pool_s, pool_t, mask, column):
    n_query, width = queries.shape
    n_pass = sum(p.shape[0] for p in pass_parts)
    pool = pool_s.shape[0]
    bf16, f32 = jnp.bfloat16, jnp.float32
    arrays = [*pass_parts, queries, teacher, pool_s, pool_t, mask, column]
    vmem = pl.BlockSpec(memory_space=pltpu.VMEM)
    return pl.pallas_call(
        functools.partial(tail_kernel, scale, len(pass_parts)),
        out_shape=[
            jax.ShapeDtypeStruct((n_query, n_pass), bf16),
            jax.ShapeDtypeStruct((n_query, pool), bf16),
            jax.ShapeDtypeStruct((n_query, 1), f32),
            jax.ShapeDtypeStruct((n_pass, width), bf16),
        ],
        in_specs=[vmem] * len(arrays),
        out_specs=[vmem] * 4,
        compiler_params=pltpu.CompilerParams(vmem_limit_bytes=VMEM_LIMIT),
        cost_estimate=pl.CostEstimate(
            flops=2 * n_query * width * (n_pass + 2 * pool),
            bytes_accessed=4 * width * (n_query + 2 * n_pass + pool),
            transcendentals=0,
        ),
        name="scores",
    )(*arrays)


def body(
    queries, teacher_queries, passages, bank_student, bank_teacher, owner, positives, keep_mask
):
    n_dev = lax.axis_size("wide")
    n_chip = n_dev // 2
    n_dp = lax.axis_size("dp")
    index = lax.axis_index("wide")
    replica = lax.axis_index("dp")
    core = index % 2
    chip = index // 2
    block, width = passages.shape
    scale = 2.0 / math.sqrt(width)
    n_pass = block * n_dev
    swap = swap_pairs(n_dev, 1)
    across = [(0, 1), (1, 0)]
    pool_s, pool_t, pass_parts = gather_rows(bank_student, bank_teacher, passages, owner[0], index, core)
    chip_of = (positives // (2 * block)) ^ chip
    core_of = ((positives // block) % 2) ^ core
    column = (core_of * n_chip + chip_of) * block + positives % block
    grad_p, grad_q, row_loss, pieces = tail(
        scale, pass_parts, queries, teacher_queries, pool_s, pool_t, keep_mask, column[:, None]
    )

    chip_bits = ["x"] + ["z%d" % b for b in range(n_chip.bit_length() - 2)]
    pairs_of = {name: swap_pairs(n_dev, 2 << b) for b, name in enumerate(chip_bits)}
    zs = chip_bits[1:]
    orders = (["x"] + zs, zs[:1] + ["x"] + zs[1:])
    lefts = [chip_bits[::-1], chip_bits[::-1]]
    sums = []
    sent = [None, None]
    mid, half = n_pass // 2, width // 2
    for h in range(2):
        columns = queries[:, h * half : (h + 1) * half]

        def terms(grads):
            return lax.dot_general(
                grads, columns, (((0,), (0,)), ((), ())), preferred_element_type=jnp.float32
            )

        got = lax.ppermute(terms(grad_p[:, mid:]).astype(jnp.bfloat16), "wide", swap)
        sums.append((terms(grad_p[:, :mid]) + got.astype(jnp.float32)).reshape((2,) * len(chip_bits) + (block, half)))
    pending = None
    for step in range(len(chip_bits)):
        for h in range(2):
            if h == 1 and step:
                pending, _ = lax.optimization_barrier((pending, sent[0]))
                sums[1] = sums[1] + pending.astype(jnp.float32)
            at = lefts[h].index(orders[h][step])
            sent[h] = lax.index_in_dim(sums[h], 1, at, keepdims=False).astype(jnp.bfloat16)
            sums[h] = lax.index_in_dim(sums[h], 0, at, keepdims=False)
            lefts[h].pop(at)
            if h == 1 and step == 0:
                sent[1], _ = lax.optimization_barrier((sent[1], sent[0]))
            if h == 0 and step == 1:
                sent[0], query_grad = lax.optimization_barrier((sent[0], query_grad))
            got = lax.ppermute(sent[h], "wide", pairs_of[orders[h][step]])
            if h == 0:
                sums[0] = sums[0] + got.astype(jnp.float32)
            else:
                pending = got
        if step == 0:
            (late_p, grad_q, row_loss), _ = lax.optimization_barrier(((grad_p, grad_q, row_loss), sent[1]))
            qgrad = jnp.dot(late_p, pieces, preferred_element_type=jnp.float32) + jnp.dot(
                grad_q, pool_s, preferred_element_type=jnp.float32
            )
            query_grad = (qgrad * scale).astype(jnp.bfloat16)
    pending, _ = lax.optimization_barrier((pending, sums[0]))
    sums[1] = sums[1] + pending.astype(jnp.float32)
    if n_dp == 2:
        sums = [x + lax.ppermute(x, "dp", across) for x in sums]
    else:
        sums = [lax.psum(x, "dp") for x in sums]
    passage_grad = jnp.concatenate(sums, 1) * scale
    return (row_loss[:, 0], query_grad, passage_grad)


def solution(mesh):
    placed = (
        P(("wide", "dp"), None),
        P(("wide", "dp"), None),
        P("wide", None),
        P("wide", None),
        P("wide", None),
        P("dp"),
        P(("wide", "dp")),
        P(("wide", "dp"), None),
    )
    return jax.shard_map(
        body,
        mesh=mesh,
        in_specs=placed,
        out_specs=(P(("wide", "dp")), P(("wide", "dp"), None), P("wide", None)),
        check_vma=False,
    )
```
